512 devices in a mesh: clip: 32 (over x, z), seq: 16 (over y, core).
Axes of the slice: x: 4, y: 8, z: 8, core: 2. Of those that a mesh axis runs over, the one named last changes fastest.
Arguments:
- queries: bfloat16 [32, 32, 64, 2560], P('clip', 'seq'), may hold values from -6 to 6
- key_rows: bfloat16 [32, 32, 64, 2560], P('clip', 'seq'), may hold values from -6 to 6
- values: bfloat16 [32, 32, 64, 2560], P('clip', 'seq'), may hold values from -6 to 6
- cotangent: bfloat16 [32, 32, 64, 2560], P('clip', 'seq'), may hold values from -6 to 6
- lengths: int32 [32], P('clip'), may hold values from 8 to 32, as said below
- episode_cuts: int32 [32, 2], P('clip'), may hold values from 1 to 31
- gain_q: float32 [2560], P('clip'), may hold values from 0.5 to 1.5
- gain_k: float32 [2560], P('clip'), may hold values from 0.5 to 1.5
Outputs:
- grad_queries: bfloat16 [32, 32, 64, 2560], P('clip', 'seq')
- grad_keys: bfloat16 [32, 32, 64, 2560], P('clip', 'seq')
- grad_values: bfloat16 [32, 32, 64, 2560], P('clip', 'seq')
- grad_gain_q: float32 [2560], P('clip')
- grad_gain_k: float32 [2560], P('clip')
The draws below stay inside these ranges and needn't reach their ends.
Inputs may be any that keep to these rules, and one draw needn't show every extreme that they name: `lengths`: frames at or past a clip's length are padding. `episode_cuts`: A cut at or past the clip's length has no effect; the two cuts of a clip may coincide.
All inputs are finite; a program needn't handle non-finite values.
Results may differ from the reference program's by a relative error of at most 0.007.
Values may be sent and summed in bfloat16 or wider, within the bound.
A program may use at most 128 MiB of HBM per device.

```python
import math
import jax
import jax.numpy as jnp
from jax import lax

HEADS = 20
HD = 128
D = 2560
P_SIZE = 64
CUTS = 2
CLIPS = 32
FRAMES = 32


def draw_lengths(key, part):
    key = jax.random.fold_in(key, 7)
    first_key, order_key = jax.random.split(key)
    drawn_len = jax.random.randint(first_key, (CLIPS,), FRAMES // 4, FRAMES + 1, dtype=jnp.int32)
    shuffled = jax.random.permutation(order_key, CLIPS)
    drawn_len = drawn_len.at[shuffled[0]].set(FRAMES).at[shuffled[1]].set(FRAMES // 4)
    return drawn_len.astype(jnp.int32)


def touch_ends(drawn, stream_key, least, high):
    longest = drawn.shape.index(max(drawn.shape))
    spots = []
    for shift in (0, 1):
        where = [jax.random.randint(jax.random.fold_in(stream_key, axis), (), 0, length) for axis, length in enumerate(drawn.shape)]
        where[longest] = (where[longest] + shift) % drawn.shape[longest]
        spots.append(tuple(where))
    return drawn.at[spots[0]].set(least).at[spots[1]].set(high)


def spiked(entries, rng, source, target, shards_of, factor):
    owner, partner = [(jnp.arange(entries.shape[axis_at]) // (entries.shape[axis_at] // shards_of)).reshape([-1 if axis == axis_at else 1 for axis in range(entries.ndim)]) for axis_at in (source, target)]
    chosen = jax.random.permutation(rng, shards_of)[partner]
    strong = (owner == chosen) | (owner == (partner + shards_of // 2) % shards_of)
    return jnp.where(strong, factor * entries, entries)


def shard_levels(rng, extent, cuts, smallest, largest):
    loudness = 1.0
    for axis_at, parts in cuts:
        heights = jax.random.uniform(jax.random.fold_in(jax.random.fold_in(rng, 6), axis_at), (parts,), jnp.float32, smallest / len(cuts), largest / len(cuts))
        loudness = loudness * jnp.repeat(jnp.exp(heights), extent[axis_at] // parts).reshape((-1,) + (1,) * (len(extent) - 1 - axis_at))
    return loudness


def centred(stream_key, shape, deviation, reach, shards=(), kind=jnp.bfloat16):
    drawn = deviation * jax.random.normal(stream_key, shape, jnp.float32)
    if shards:
        drawn = drawn * shard_levels(stream_key, shape, shards, -0.22, 0.18)
    return jnp.clip(drawn, -reach, reach).astype(kind)


def gaussian_with(key, shape, scale, bound, pieces, heavy, kind=jnp.bfloat16):
    entries = scale * jax.random.normal(key, shape, jnp.float32)
    if pieces:
        entries = entries * shard_levels(key, shape, pieces, -0.22, 0.18)
    return jnp.clip(spiked(entries, jax.random.fold_in(key, 3), *heavy), -bound, bound).astype(kind)


def setup_inputs(seed: int = 0) -> dict:
    keys = jax.random.split(jax.random.key(seed), 9)
    return {
        "queries": centred(keys[0], (CLIPS, FRAMES, P_SIZE, D), 1.0, 6.0, ((0, 32), (1, 16))),
        "key_rows": centred(keys[1], (CLIPS, FRAMES, P_SIZE, D), 1.0, 6.0, ((0, 32), (1, 16))),
        "values": centred(keys[2], (CLIPS, FRAMES, P_SIZE, D), 1.0, 6.0, ((0, 32), (1, 16))),
        "cotangent": gaussian_with(keys[3], (CLIPS, FRAMES, P_SIZE, D), 1.0, 6.0, ((0, 32), (1, 16)), (0, 3, 32, 2.75)),
        "lengths": draw_lengths(jax.random.fold_in(keys[8], 71), 0),
        "episode_cuts": touch_ends(jax.random.randint(keys[5], (CLIPS, CUTS), 1, FRAMES), jax.random.fold_in(keys[5], 1), 1, FRAMES - 1).astype(jnp.int32),
        "gain_q": jnp.clip(1.0 + 0.1 * jax.random.normal(keys[6], (D,), jnp.float32), 0.5, 1.5),
        "gain_k": jnp.clip(1.0 + 0.1 * jax.random.normal(keys[7], (D,), jnp.float32), 0.5, 1.5),
    }


EPS = 1e-06

def rounded(array):
    return lax.optimization_barrier(array.astype(jnp.bfloat16)).astype(jnp.float32)

def clip_grads(query_rows, key_block, value_rows, grad_rows, length, clip_cuts, gain_q, gain_k):
    frame_count = query_rows.shape[0]
    patch_count = query_rows.shape[1]
    split_shape = (frame_count, patch_count, HEADS, HD)
    q_values = query_rows.astype(jnp.float32).reshape(split_shape)
    k_values = key_block.astype(jnp.float32).reshape(split_shape)
    v_values = value_rows.astype(jnp.float32).reshape(split_shape)
    g_values = grad_rows.astype(jnp.float32).reshape(split_shape)
    q_gain = gain_q.reshape(HEADS, HD)
    k_gain = gain_k.reshape(HEADS, HD)
    q_inv = lax.rsqrt(lax.optimization_barrier(jnp.mean(q_values * q_values, axis=-1, keepdims=True)) + EPS)
    k_inv = lax.rsqrt(lax.optimization_barrier(jnp.mean(k_values * k_values, axis=-1, keepdims=True)) + EPS)
    q_normed = rounded(q_values * q_inv * q_gain)
    k_normed = rounded(k_values * k_inv * k_gain)
    score_scale = 1.0 / math.sqrt(HD)
    frame_ids = jnp.arange(frame_count, dtype=jnp.int32)
    episode = lax.optimization_barrier(jnp.sum((clip_cuts[None, :] <= frame_ids[:, None]).astype(jnp.int32), axis=1))
    live_frames = frame_ids < length
    visible = (frame_ids[None, :] <= frame_ids[:, None]) & (episode[None, :] == episode[:, None]) & live_frames[:, None]
    scores = jnp.einsum('tphd,sphd->phts', q_normed, k_normed) * score_scale
    exps = jnp.where(visible, jnp.exp(scores), 0.0)
    denominator = lax.optimization_barrier(jnp.sum(exps, axis=-1, keepdims=True)) + (1.0 - live_frames.astype(jnp.float32))[:, None]
    softmax = exps / denominator
    soft_round = rounded(softmax)
    attended = jnp.einsum('phts,sphd->tphd', soft_round, v_values)
    row_delta = lax.optimization_barrier(jnp.sum(g_values * attended, axis=-1))
    dprob = jnp.einsum('tphd,sphd->phts', g_values, v_values)
    dscore = softmax * (dprob - jnp.transpose(row_delta, (1, 2, 0))[..., None])
    ds_round = rounded(dscore)
    dq_normed = jnp.einsum('phts,sphd->tphd', ds_round, k_normed) * score_scale
    dk_normed = jnp.einsum('phts,tphd->sphd', ds_round, q_normed) * score_scale
    dv_rows = jnp.einsum('phts,tphd->sphd', soft_round, g_values)
    q_scaled = q_gain * dq_normed
    dq_rows = q_inv * q_scaled - q_values * q_inv ** 3 * lax.optimization_barrier(jnp.mean(q_values * q_scaled, axis=-1, keepdims=True))
    k_scaled = k_gain * dk_normed
    dk_rows = k_inv * k_scaled - k_values * k_inv ** 3 * lax.optimization_barrier(jnp.mean(k_values * k_scaled, axis=-1, keepdims=True))
    part_q = lax.optimization_barrier(jnp.sum(q_values * q_inv * dq_normed, axis=(0, 1))).reshape(-1)
    part_k = lax.optimization_barrier(jnp.sum(k_values * k_inv * dk_normed, axis=(0, 1))).reshape(-1)
    flat_shape = (frame_count, patch_count, HEADS * HD)
    return (dq_rows.reshape(flat_shape).astype(jnp.bfloat16), dk_rows.reshape(flat_shape).astype(jnp.bfloat16), dv_rows.reshape(flat_shape).astype(jnp.bfloat16), part_q, part_k)

def reference(queries, key_rows, values, cotangent, lengths, episode_cuts, gain_q, gain_k):

    def one_clip(items):
        return clip_grads(items[0], items[1], items[2], items[3], items[4], items[5], gain_q, gain_k)
    grad_q, grad_k, grad_v, parts_q, parts_k = lax.map(one_clip, (queries, key_rows, values, cotangent, lengths, episode_cuts))
    return (grad_q, grad_k, grad_v, lax.optimization_barrier(jnp.sum(parts_q, axis=0)), lax.optimization_barrier(jnp.sum(parts_k, axis=0)))
```

```python
import math

import jax
import jax.numpy as jnp
from jax import lax
from jax.experimental import pallas as pl
from jax.experimental.pallas import tpu as pltpu
from jax.sharding import PartitionSpec as P

HEADS = 20
HD = 128
EPS = 1e-06
FRAMES = 32
XS = 4
ZS = 8
SEQ = 16
OWN = FRAMES // SEQ
TILE = 16
PATCHES = 64
TILES = PATCHES // TILE
GROUPS = SEQ // TILES
GH = HEADS // GROUPS
ROWS = FRAMES * TILE
BLK = 128
NBLK = ROWS // BLK
BF = BLK // TILE
SLICE = HEADS * HD // (XS * ZS)
MESH = pl.DeviceIdType.MESH
F32 = jnp.float32
BF16 = jnp.bfloat16


def lanes(array, start):
    row, off = divmod(start, HD)
    first = array(row)
    if off == 0:
        return first
    low = pltpu.roll(first, HD - off, 1)
    if row + 1 >= GH:
        return low
    high = pltpu.roll(array(row + 1), HD - off, 1)
    lane = lax.broadcasted_iota(jnp.int32, first.shape, 1)
    return jnp.where(lane < HD - off, low, high)


def kernel(
    len_ref, cut_ref, gq_ref, gk_ref, q_hbm, k_hbm, v_hbm, g_hbm,
    o_hbm, gain_out,
    stage, recv, obuf, qh_s, kh_s, soft_s, ds_s, bias, gains, parts,
    gsend, grecv, psend, precv, fsend, frecv,
    stage_sem, send_sem, recv_sem, osend_sem, orecv_sem,
    gsend_sem, grecv_sem, psend_sem, precv_sem, fsend_sem, frecv_sem,
):
    clip = lax.axis_index("clip")
    me = lax.axis_index("seq")
    x, z = lax.div(clip, ZS), lax.rem(clip, ZS)
    g, j = lax.div(me, TILES), lax.rem(me, TILES)
    far_seq = x * TILES + j
    same = (g == x).astype(jnp.int32)

    def far(zz):
        return (g * ZS + zz, far_seq)

    def is_me(zz):
        return jnp.logical_and(g == x, z == zz)

    for n, ref in enumerate((q_hbm, k_hbm, v_hbm, g_hbm)):
        pltpu.make_async_copy(ref, stage.at[n], stage_sem).start()

    barrier = pltpu.get_barrier_semaphore()
    for d in range(1, SEQ):
        pl.semaphore_signal(
            barrier, inc=1, device_id=(clip, lax.rem(me + d, SEQ)), device_id_type=MESH
        )
    for zz in range(ZS):

        @pl.when(jnp.logical_not(is_me(zz)))
        def _():
            pl.semaphore_signal(barrier, inc=1, device_id=far(zz), device_id_type=MESH)

    gsend[...] = jnp.zeros_like(gsend)
    gsend[0:1, 0:SLICE] = gq_ref[...]
    gsend[1:2, 0:SLICE] = gk_ref[...]

    def exchange(src, dst, s_sem, r_sem):
        for zz in range(ZS):

            @pl.when(is_me(zz))
            def _():
                pltpu.make_async_copy(src(zz), dst.at[z], r_sem).start()

            @pl.when(jnp.logical_not(is_me(zz)))
            def _():
                pltpu.make_async_remote_copy(
                    src_ref=src(zz), dst_ref=dst.at[z], send_sem=s_sem, recv_sem=r_sem,
                    device_id=far(zz), device_id_type=MESH,
                ).start()

    def exchange_sent(dst, s_sem):
        @pl.when(same == 1)
        def _():
            part = dst.at[pl.ds(0, ZS - 1)]
            pltpu.make_async_copy(part, part, s_sem).wait()

        @pl.when(same == 0)
        def _():
            pltpu.make_async_copy(dst, dst, s_sem).wait()

    pltpu.make_async_copy(stage, stage, stage_sem).wait()
    pl.semaphore_wait(barrier, SEQ - 1 + ZS - same)

    exchange(lambda zz: gsend, grecv, gsend_sem, grecv_sem)

    def send_in(h, _):
        def source(to):
            to_g, to_j = lax.div(to, TILES), lax.rem(to, TILES)
            return stage.at[
                :, :, pl.ds(pl.multiple_of(to_j * TILE, TILE), TILE),
                pl.ds(pl.multiple_of((to_g * GH + h) * HD, HD), HD),
            ]

        place = recv.at[h, :, pl.ds(me * OWN, OWN)]
        for d in range(1, SEQ):
            to = lax.rem(me + d, SEQ)
            pltpu.make_async_remote_copy(
                src_ref=source(to), dst_ref=place, send_sem=send_sem, recv_sem=recv_sem.at[h],
                device_id=(clip, to), device_id_type=MESH,
            ).start()
        pltpu.make_async_copy(source(me), place, recv_sem.at[h]).start()
        return 0

    lax.fori_loop(0, GH, send_in, 0)

    length = len_ref[0]
    cut_a, cut_b = cut_ref[0, 0], cut_ref[0, 1]
    for tb in range(NBLK):
        rows = BLK * (tb + 1)
        s_at = lax.broadcasted_iota(jnp.int32, (rows, BLK), 0)
        t_at = lax.broadcasted_iota(jnp.int32, (rows, BLK), 1) + tb * BLK
        s_f, t_f = s_at // TILE, t_at // TILE
        s_e = (cut_a <= s_f).astype(jnp.int32) + (cut_b <= s_f).astype(jnp.int32)
        t_e = (cut_a <= t_f).astype(jnp.int32) + (cut_b <= t_f).astype(jnp.int32)
        ok = (s_f <= t_f) & (s_e == t_e) & (t_f < length) & (s_at % TILE == t_at % TILE)
        bias[0:rows, tb * BLK : (tb + 1) * BLK] = jnp.where(ok, 0.0, -1e30)

    pltpu.make_async_copy(grecv, grecv, grecv_sem).wait()
    gains[...] = jnp.zeros_like(gains)
    for zz in range(ZS):
        row, off = divmod(zz * SLICE, HD)
        for n in range(2):
            piece = grecv[zz, n : n + 1, :]
            moved = pltpu.roll(piece, off, 1) if off else piece
            lane = lax.broadcasted_iota(jnp.int32, (1, HD), 1)
            gains[n, row : row + 1, :] += jnp.where(lane >= off, moved, 0.0)
            if off + SLICE > HD:
                gains[n, row + 1 : row + 2, :] += jnp.where(lane < off + SLICE - HD, moved, 0.0)

    scale = 1.0 / math.sqrt(HD)
    along = (((1,), (1,)), ((), ()))
    down = (((0,), (0,)), ((), ()))
    plain = (((1,), (0,)), ((), ()))

    def dot(a, b, dims):
        return lax.dot_general(a, b, dims, preferred_element_type=F32)

    def mean(a):
        return jnp.sum(a, axis=-1, keepdims=True) * (1.0 / HD)

    def flat(ref, lo, hi):
        return ref[lo // TILE : hi // TILE].reshape(hi - lo, HD)

    def restore(raw, inv, gain, grad, n, h, lo):
        scaled = gain * grad
        normed = raw * inv
        out = inv * (scaled - normed * mean(normed * scaled))
        obuf[h, n, lo // TILE : (lo + BLK) // TILE] = out.astype(BF16).reshape(BF, TILE, HD)
        return jnp.sum(normed * grad, axis=0, keepdims=True)

    def head(h, _):
        pltpu.make_async_copy(recv.at[h], recv.at[h], recv_sem.at[h]).wait()
        q_r, k_r, v_r, g_r = (recv.at[h, n] for n in range(4))
        gain_q = gains[0, pl.ds(h, 1), :]
        gain_k = gains[1, pl.ds(h, 1), :]
        inv_q, inv_k = [], []
        for b in range(NBLK):
            lo, hi = b * BLK, (b + 1) * BLK
            for src, invs, gain, dst in ((q_r, inv_q, gain_q, qh_s), (k_r, inv_k, gain_k, kh_s)):
                raw = flat(src, lo, hi).astype(F32)
                inv = lax.rsqrt(mean(raw * raw) + EPS)
                invs.append(inv)
                dst[lo:hi] = (raw * inv * gain).astype(BF16)

        part_q = jnp.zeros((1, HD), F32)
        part_k = jnp.zeros((1, HD), F32)
        for b in range(NBLK):
            lo, hi = b * BLK, (b + 1) * BLK
            scores = dot(kh_s[0:hi], qh_s[lo:hi], along)
            exps = jnp.exp(scores * scale + bias[0:hi, lo:hi])
            frame = (lax.broadcasted_iota(jnp.int32, (1, BLK), 1) + lo) // TILE
            dead = (frame >= length).astype(F32)
            total = jnp.sum(exps, axis=0, keepdims=True) + dead
            soft = exps * (1.0 / total)
            soft_b = soft.astype(BF16)
            dprob = dot(flat(v_r, 0, hi), flat(g_r, lo, hi), along)
            delta = jnp.sum(soft_b.astype(F32) * dprob, axis=0, keepdims=True)
            ds_b = (soft * (dprob - delta)).astype(BF16)
            soft_s[0:hi, lo:hi] = soft_b
            ds_s[0:hi, lo:hi] = ds_b
            dq = dot(ds_b, kh_s[0:hi], down) * scale
            raw = flat(q_r, lo, hi).astype(F32)
            part_q += restore(raw, inv_q[b], gain_q, dq, 0, h, lo)
        for b in range(NBLK):
            lo, hi = b * BLK, (b + 1) * BLK
            dk = dot(ds_s[lo:hi, lo:ROWS], qh_s[lo:ROWS], plain) * scale
            raw = flat(k_r, lo, hi).astype(F32)
            part_k += restore(raw, inv_k[b], gain_k, dk, 1, h, lo)
            dv = dot(soft_s[lo:hi, lo:ROWS], flat(g_r, lo, ROWS), plain)
            obuf[h, 2, lo // TILE : hi // TILE] = dv.astype(BF16).reshape(BF, TILE, HD)
        parts[0, pl.ds(h, 1), :] = part_q
        parts[1, pl.ds(h, 1), :] = part_k

        place = o_hbm.at[
            :, :, pl.ds(pl.multiple_of(j * TILE, TILE), TILE),
            pl.ds(pl.multiple_of((g * GH + h) * HD, HD), HD),
        ]
        for d in range(1, SEQ):
            to = lax.rem(me + d, SEQ)
            pltpu.make_async_remote_copy(
                src_ref=obuf.at[h, :, pl.ds(to * OWN, OWN)], dst_ref=place,
                send_sem=osend_sem, recv_sem=orecv_sem,
                device_id=(clip, to), device_id_type=MESH,
            ).start()
        pltpu.make_async_copy(obuf.at[h, :, pl.ds(me * OWN, OWN)], place, orecv_sem).start()
        return 0

    lax.fori_loop(0, GH, head, 0)

    for zz in range(ZS):
        for n in range(2):
            psend[zz, n : n + 1, :] = lanes(lambda r: parts[n, r : r + 1, :], zz * SLICE)
    exchange(lambda zz: psend.at[zz], precv, psend_sem, precv_sem)
    pltpu.make_async_copy(precv, precv, precv_sem).wait()
    fsend[...] = jnp.sum(precv[...], axis=0)
    for d in range(1, SEQ):
        pltpu.make_async_remote_copy(
            src_ref=fsend, dst_ref=frecv.at[me], send_sem=fsend_sem, recv_sem=frecv_sem,
            device_id=(clip, lax.rem(me + d, SEQ)), device_id_type=MESH,
        ).start()
    pltpu.make_async_copy(fsend, frecv.at[me], frecv_sem).start()
    pltpu.make_async_copy(frecv, frecv, frecv_sem).wait()
    gain_out[...] = jnp.sum(frecv[...], axis=0)

    pltpu.make_async_copy(o_hbm, o_hbm, orecv_sem).wait()
    exchange_sent(grecv, gsend_sem)
    exchange_sent(precv, psend_sem)
    sent = frecv.at[pl.ds(0, SEQ - 1)]
    pltpu.make_async_copy(sent, sent, fsend_sem).wait()
    sent = recv.at[:, :, pl.ds(0, FRAMES - OWN)]
    pltpu.make_async_copy(sent, sent, send_sem).wait()
    sent = obuf.at[:, :, pl.ds(0, FRAMES - OWN)]
    pltpu.make_async_copy(sent, sent, osend_sem).wait()


def body(queries, key_rows, values, cotangent, lengths, episode_cuts, gain_q, gain_k):
    smem = pl.BlockSpec(memory_space=pltpu.SMEM)
    vmem = pl.BlockSpec(memory_space=pltpu.VMEM)
    hbm = pl.BlockSpec(memory_space=pl.ANY)
    dma = pltpu.SemaphoreType.DMA
    width = HEADS * HD
    out, gain = pl.pallas_call(
        kernel,
        out_shape=(
            jax.ShapeDtypeStruct((3, OWN, PATCHES, width), BF16),
            jax.ShapeDtypeStruct((2, HD), F32),
        ),
        in_specs=[smem, smem, vmem, vmem, hbm, hbm, hbm, hbm],
        out_specs=(hbm, vmem),
        scratch_shapes=[
            pltpu.VMEM((4, OWN, PATCHES, width), BF16),
            pltpu.VMEM((GH, 4, FRAMES, TILE, HD), BF16),
            pltpu.VMEM((GH, 3, FRAMES, TILE, HD), BF16),
            pltpu.VMEM((ROWS, HD), BF16),
            pltpu.VMEM((ROWS, HD), BF16),
            pltpu.VMEM((ROWS, ROWS), BF16),
            pltpu.VMEM((ROWS, ROWS), BF16),
            pltpu.VMEM((ROWS, ROWS), F32),
            pltpu.VMEM((2, 8, HD), F32),
            pltpu.VMEM((2, 8, HD), F32),
            pltpu.VMEM((2, HD), F32),
            pltpu.VMEM((ZS, 2, HD), F32),
            pltpu.VMEM((ZS, 2, HD), F32),
            pltpu.VMEM((ZS, 2, HD), F32),
            pltpu.VMEM((2, HD), F32),
            pltpu.VMEM((SEQ, 2, HD), F32),
            dma, dma, dma((GH,)), dma, dma,
            dma, dma, dma, dma, dma, dma,
        ],
        compiler_params=pltpu.CompilerParams(
            collective_id=0, has_side_effects=True, vmem_limit_bytes=40 * 2**20
        ),
    )(
        lengths, episode_cuts, gain_q.reshape(1, SLICE), gain_k.reshape(1, SLICE),
        *(a.reshape(OWN, PATCHES, width) for a in (queries, key_rows, values, cotangent)),
    )
    return (out[0][None], out[1][None], out[2][None], gain[0, :SLICE], gain[1, :SLICE])


def solution(mesh):
    rows = P("clip", "seq", None, None)
    return jax.shard_map(
        body,
        mesh=mesh,
        in_specs=(rows, rows, rows, rows, P("clip"), P("clip", None), P("clip"), P("clip")),
        out_specs=(rows, rows, rows, P("clip"), P("clip")),
        check_vma=False,
    )
```

```python
import math

import jax
import jax.numpy as jnp
from jax import lax
from jax.experimental import pallas as pl
from jax.experimental.pallas import tpu as pltpu
from jax.sharding import PartitionSpec as P

HEADS = 20
HD = 128
EPS = 1e-06
FRAMES = 32
XS = 4
ZS = 8
SEQ = 16
OWN = FRAMES // SEQ
TILE = 16
PATCHES = 64
TILES = PATCHES // TILE
GROUPS = SEQ // TILES
GH = HEADS // GROUPS
ROWS = FRAMES * TILE
BLK = 128
NBLK = ROWS // BLK
BF = BLK // TILE
SLICE = HEADS * HD // (XS * ZS)
MESH = pl.DeviceIdType.MESH
F32 = jnp.float32
BF16 = jnp.bfloat16


def lanes(array, start):
    row, off = divmod(start, HD)
    first = array(row)
    if off == 0:
        return first
    low = pltpu.roll(first, HD - off, 1)
    if row + 1 >= GH:
        return low
    high = pltpu.roll(array(row + 1), HD - off, 1)
    lane = lax.broadcasted_iota(jnp.int32, first.shape, 1)
    return jnp.where(lane < HD - off, low, high)


PEERS = [(dy, dc) for dy in (4, 3, -3, 2, -2, 1, -1) for dc in (0, 1)] + [(0, 1)]
EARLY = 2


def kernel(
    len_hbm, cut_hbm, gq_hbm, gk_hbm, q_hbm, k_hbm, v_hbm, g_hbm,
    o_ref, gain_out,
    len_ref, cut_ref, gq_ref, gk_ref,
    stage, recv, obuf, qh_s, kh_s, soft_s, ds_s, bias, gains, parts,
    gsend, gmid, grecv, psend, precv, asend, brecv, csend, crecv,
    small_sem, stage_sem, send_sem, recv_sem, osend_sem, orecv_sem,
    gsend_sem, gmid_sem, hsend_sem, grecv_sem,
    asend_sem, arecv_sem, bsend_sem, brecv_sem, csend_sem, crecv_sem,
):
    clip = lax.axis_index("clip")
    me = lax.axis_index("seq")
    x, z = lax.div(clip, ZS), lax.rem(clip, ZS)
    g, j = lax.div(me, TILES), lax.rem(me, TILES)
    y, core = lax.div(me, 2), lax.rem(me, 2)
    home = g == x

    def seq_peer(n):
        dy, dc = PEERS[n]
        return lax.rem(y + (dy + 8), 8) * 2 + lax.rem(core + dc, 2)

    def at_x(xx):
        return (xx * ZS + z, me)

    def at_z(zz):
        return (x * ZS + zz, me)

    def remote(src, dst, s_sem, r_sem, to):
        pltpu.make_async_remote_copy(
            src_ref=src, dst_ref=dst, send_sem=s_sem, recv_sem=r_sem,
            device_id=to, device_id_type=MESH,
        ).start()

    def done(ref, sem):
        pltpu.make_async_copy(ref, ref, sem).wait()

    small = [
        pltpu.make_async_copy(a, b, small_sem.at[n])
        for n, (a, b) in enumerate(
            ((gq_hbm, gq_ref), (gk_hbm, gk_ref), (len_hbm, len_ref), (cut_hbm, cut_ref))
        )
    ]
    barrier = pltpu.get_barrier_semaphore()
    others = [(clip, seq_peer(n)) for n in range(SEQ - 1)]
    others += [at_x(lax.rem(x + d, XS)) for d in range(1, XS)]
    others += [at_z(lax.rem(z + d, ZS)) for d in range(1, ZS)]
    for to in others:
        pl.semaphore_signal(barrier, inc=1, device_id=to, device_id_type=MESH)
    for n, ref in enumerate((q_hbm, k_hbm, v_hbm, g_hbm)):
        pltpu.make_async_copy(ref, stage.at[n], stage_sem).start()
    for copy in small:
        copy.start()
    for copy in small:
        copy.wait()

    gsend[...] = jnp.zeros_like(gsend)
    gsend[0:1, 0:SLICE] = gq_ref[...]
    gsend[1:2, 0:SLICE] = gk_ref[...]
    done(stage, stage_sem)
    pl.semaphore_wait(barrier, len(others))

    @pl.when(home)
    def _():
        for d in range(1, XS):
            remote(gsend, gmid, gsend_sem, gmid_sem, at_x(lax.rem(x + d, XS)))

    def send_in(h):
        def source(to):
            to_g, to_j = lax.div(to, TILES), lax.rem(to, TILES)
            return stage.at[
                :, :, pl.ds(pl.multiple_of(to_j * TILE, TILE), TILE),
                pl.ds(pl.multiple_of((to_g * GH + h) * HD, HD), HD),
            ]

        place = recv.at[h, :, pl.ds(me * OWN, OWN)]
        for n in range(SEQ - 1):
            to = seq_peer(n)
            remote(source(to), place, send_sem, recv_sem.at[h], (clip, to))
        pltpu.make_async_copy(source(me), place, recv_sem.at[h]).start()

    def loop(lo, hi, step):
        def run(h, _):
            step(h)
            return 0

        lax.fori_loop(lo, hi, run, 0)

    loop(0, 2, send_in)

    @pl.when(home)
    def _():
        gmid[...] = gsend[...]

    @pl.when(jnp.logical_not(home))
    def _():
        done(gmid, gmid_sem)

    for d in range(1, ZS):
        remote(gmid, grecv.at[z], hsend_sem, grecv_sem, at_z(lax.rem(z + d, ZS)))
    pltpu.make_async_copy(gmid, grecv.at[z], grecv_sem).start()

    loop(2, GH, send_in)

    length = len_ref[0]
    cut_a, cut_b = cut_ref[0, 0], cut_ref[0, 1]
    for tb in range(NBLK):
        rows = BLK * (tb + 1)
        s_at = lax.broadcasted_iota(jnp.int32, (rows, BLK), 0)
        t_at = lax.broadcasted_iota(jnp.int32, (rows, BLK), 1) + tb * BLK
        s_f, t_f = s_at // TILE, t_at // TILE
        s_e = (cut_a <= s_f).astype(jnp.int32) + (cut_b <= s_f).astype(jnp.int32)
        t_e = (cut_a <= t_f).astype(jnp.int32) + (cut_b <= t_f).astype(jnp.int32)
        ok = (s_f <= t_f) & (s_e == t_e) & (t_f < length) & (s_at % TILE == t_at % TILE)
        bias[0:rows, tb * BLK : (tb + 1) * BLK] = jnp.where(ok, 0.0, -1e30)

    done(grecv, grecv_sem)
    gains[...] = jnp.zeros_like(gains)
    for zz in range(ZS):
        row, off = divmod(zz * SLICE, HD)
        for n in range(2):
            piece = grecv[zz, n : n + 1, :]
            moved = pltpu.roll(piece, off, 1) if off else piece
            lane = lax.broadcasted_iota(jnp.int32, (1, HD), 1)
            gains[n, row : row + 1, :] += jnp.where(lane >= off, moved, 0.0)
            if off + SLICE > HD:
                gains[n, row + 1 : row + 2, :] += jnp.where(lane < off + SLICE - HD, moved, 0.0)

    scale = 1.0 / math.sqrt(HD)
    along = (((1,), (1,)), ((), ()))
    down = (((0,), (0,)), ((), ()))
    plain = (((1,), (0,)), ((), ()))

    def dot(a, b, dims):
        return lax.dot_general(a, b, dims, preferred_element_type=F32)

    def mean(a):
        return jnp.sum(a, axis=-1, keepdims=True) * (1.0 / HD)

    def flat(ref, lo, hi):
        return ref[lo // TILE : hi // TILE].reshape(hi - lo, HD)

    def restore(raw, inv, gain, grad, n, h, lo):
        scaled = gain * grad
        normed = raw * inv
        out = inv * (scaled - normed * mean(normed * scaled))
        obuf[h, n, lo // TILE : (lo + BLK) // TILE] = out.astype(BF16).reshape(BF, TILE, HD)
        return jnp.sum(normed * grad, axis=0, keepdims=True)

    def head(h):
        done(recv.at[h], recv_sem.at[h])
        q_r, k_r, v_r, g_r = (recv.at[h, n] for n in range(4))
        gain_q = gains[0, pl.ds(h, 1), :]
        gain_k = gains[1, pl.ds(h, 1), :]
        inv_q, inv_k = [], []
        for b in range(NBLK):
            lo, hi = b * BLK, (b + 1) * BLK
            for src, invs, gain, dst in ((q_r, inv_q, gain_q, qh_s), (k_r, inv_k, gain_k, kh_s)):
                raw = flat(src, lo, hi).astype(F32)
                inv = lax.rsqrt(mean(raw * raw) + EPS)
                invs.append(inv)
                dst[lo:hi] = (raw * inv * gain).astype(BF16)

        part_q = jnp.zeros((1, HD), F32)
        part_k = jnp.zeros((1, HD), F32)
        for b in range(NBLK):
            lo, hi = b * BLK, (b + 1) * BLK
            scores = dot(kh_s[0:hi], qh_s[lo:hi], along)
            exps = jnp.exp(scores * scale + bias[0:hi, lo:hi])
            frame = (lax.broadcasted_iota(jnp.int32, (1, BLK), 1) + lo) // TILE
            dead = (frame >= length).astype(F32)
            total = jnp.sum(exps, axis=0, keepdims=True) + dead
            soft = exps * (1.0 / total)
            soft_b = soft.astype(BF16)
            dprob = dot(flat(v_r, 0, hi), flat(g_r, lo, hi), along)
            delta = jnp.sum(soft_b.astype(F32) * dprob, axis=0, keepdims=True)
            ds_b = (soft * (dprob - delta)).astype(BF16)
            soft_s[0:hi, lo:hi] = soft_b
            ds_s[0:hi, lo:hi] = ds_b
            dq = dot(ds_b, kh_s[0:hi], down) * scale
            raw = flat(q_r, lo, hi).astype(F32)
            part_q += restore(raw, inv_q[b], gain_q, dq, 0, h, lo)
        for b in range(NBLK):
            lo, hi = b * BLK, (b + 1) * BLK
            dk = dot(ds_s[lo:hi, lo:ROWS], qh_s[lo:ROWS], plain) * scale
            raw = flat(k_r, lo, hi).astype(F32)
            part_k += restore(raw, inv_k[b], gain_k, dk, 1, h, lo)
            dv = dot(soft_s[lo:hi, lo:ROWS], flat(g_r, lo, ROWS), plain)
            obuf[h, 2, lo // TILE : hi // TILE] = dv.astype(BF16).reshape(BF, TILE, HD)
        parts[0, pl.ds(h, 1), :] = part_q
        parts[1, pl.ds(h, 1), :] = part_k

        @pl.when(h < EARLY)
        def _():
            send_out(h)

    def send_out(h):
        place = o_ref.at[
            :, :, pl.ds(pl.multiple_of(j * TILE, TILE), TILE),
            pl.ds(pl.multiple_of((g * GH + h) * HD, HD), HD),
        ]
        for n in range(SEQ - 1):
            to = seq_peer(n)
            remote(
                obuf.at[h, :, pl.ds(to * OWN, OWN)], place, osend_sem, orecv_sem, (clip, to)
            )
        pltpu.make_async_copy(obuf.at[h, :, pl.ds(me * OWN, OWN)], place, orecv_sem).start()

    loop(0, GH, head)

    for zz in range(ZS):
        for n in range(2):
            psend[zz, n : n + 1, :] = lanes(lambda r: parts[n, r : r + 1, :], zz * SLICE)
    for d in range(1, ZS):
        zz = lax.rem(z + d, ZS)
        remote(psend.at[zz], precv.at[z], asend_sem, arecv_sem, at_z(zz))
    pltpu.make_async_copy(psend.at[z], precv.at[z], arecv_sem).start()
    send_out(EARLY)
    done(precv, arecv_sem)
    asend[...] = jnp.sum(precv[...], axis=0)

    @pl.when(home)
    def _():
        pltpu.make_async_copy(asend, brecv.at[x], brecv_sem).start()

    @pl.when(jnp.logical_not(home))
    def _():
        remote(asend, brecv.at[x], bsend_sem, brecv_sem, at_x(g))

    send_out(EARLY + 1)

    @pl.when(home)
    def _():
        done(brecv, brecv_sem)
        csend[...] = jnp.sum(brecv[...], axis=0)
        for n in range(SEQ - 1):
            remote(csend, crecv.at[j], csend_sem, crecv_sem, (clip, seq_peer(n)))
        pltpu.make_async_copy(csend, crecv.at[j], crecv_sem).start()

    send_out(EARLY + 2)
    done(crecv.at[pl.ds(0, TILES)], crecv_sem)
    gain_out[...] = jnp.sum(crecv[0:TILES], axis=0)

    @pl.when(home)
    def _():
        done(brecv.at[pl.ds(0, XS - 1)], gsend_sem)
        done(crecv.at[pl.ds(0, SEQ - 1)], csend_sem)

    @pl.when(jnp.logical_not(home))
    def _():
        done(asend, bsend_sem)

    done(grecv.at[pl.ds(0, ZS - 1)], hsend_sem)
    done(precv.at[pl.ds(0, ZS - 1)], asend_sem)
    done(recv.at[:, :, pl.ds(0, FRAMES - OWN)], send_sem)
    done(obuf.at[:, :, pl.ds(0, FRAMES - OWN)], osend_sem)
    done(o_ref, orecv_sem)


def body(queries, key_rows, values, cotangent, lengths, episode_cuts, gain_q, gain_k):
    vmem = pl.BlockSpec(memory_space=pltpu.VMEM)
    hbm = pl.BlockSpec(memory_space=pltpu.HBM)
    dma = pltpu.SemaphoreType.DMA
    width = HEADS * HD
    row = pltpu.VMEM((2, HD), F32)
    out, gain = pl.pallas_call(
        kernel,
        out_shape=(
            jax.ShapeDtypeStruct((3, OWN, PATCHES, width), BF16),
            jax.ShapeDtypeStruct((2, HD), F32),
        ),
        in_specs=[hbm] * 8,
        out_specs=(hbm, vmem),
        scratch_shapes=[
            pltpu.SMEM((1,), jnp.int32),
            pltpu.SMEM((1, 2), jnp.int32),
            pltpu.VMEM((1, SLICE), F32),
            pltpu.VMEM((1, SLICE), F32),
            pltpu.VMEM((4, OWN, PATCHES, width), BF16),
            pltpu.VMEM((GH, 4, FRAMES, TILE, HD), BF16),
            pltpu.VMEM((GH, 3, FRAMES, TILE, HD), BF16),
            pltpu.VMEM((ROWS, HD), BF16),
            pltpu.VMEM((ROWS, HD), BF16),
            pltpu.VMEM((ROWS, ROWS), BF16),
            pltpu.VMEM((ROWS, ROWS), BF16),
            pltpu.VMEM((ROWS, ROWS), F32),
            pltpu.VMEM((2, 8, HD), F32),
            pltpu.VMEM((2, 8, HD), F32),
            row,
            row,
            pltpu.VMEM((ZS, 2, HD), F32),
            pltpu.VMEM((ZS, 2, HD), F32),
            pltpu.VMEM((ZS, 2, HD), F32),
            row,
            pltpu.VMEM((XS, 2, HD), F32),
            row,
            pltpu.VMEM((SEQ, 2, HD), F32),
            dma((4,)), dma, dma, dma((GH,)), dma, dma,
            dma, dma, dma, dma,
            dma, dma, dma, dma, dma, dma,
        ],
        compiler_params=pltpu.CompilerParams(
            collective_id=0, has_side_effects=True, vmem_limit_bytes=60 * 2**20
        ),
    )(
        lengths, episode_cuts, gain_q.reshape(1, SLICE), gain_k.reshape(1, SLICE),
        *(a.reshape(OWN, PATCHES, width) for a in (queries, key_rows, values, cotangent)),
    )
    return (out[0][None], out[1][None], out[2][None], gain[0, :SLICE], gain[1, :SLICE])


def solution(mesh):
    rows = P("clip", "seq", None, None)
    return jax.shard_map(
        body,
        mesh=mesh,
        in_specs=(rows, rows, rows, rows, P("clip"), P("clip", None), P("clip"), P("clip")),
        out_specs=(rows, rows, rows, P("clip"), P("clip")),
        check_vma=False,
    )
```

```python
import math

import jax
import jax.numpy as jnp
from jax import lax
from jax.experimental import pallas as pl
from jax.experimental.pallas import tpu as pltpu
from jax.sharding import PartitionSpec as P

HEADS = 20
HD = 128
EPS = 1e-06
FRAMES = 32
XS = 4
ZS = 8
SEQ = 16
OWN = FRAMES // SEQ
TILE = 16
PATCHES = 64
TILES = PATCHES // TILE
GROUPS = SEQ // TILES
GH = HEADS // GROUPS
ROWS = FRAMES * TILE
BLK = 128
NBLK = ROWS // BLK
BF = BLK // TILE
SLICE = HEADS * HD // (XS * ZS)
MESH = pl.DeviceIdType.MESH
F32 = jnp.float32
BF16 = jnp.bfloat16


def lanes(array, start):
    row, off = divmod(start, HD)
    first = array(row)
    if off == 0:
        return first
    low = pltpu.roll(first, HD - off, 1)
    if row + 1 >= GH:
        return low
    high = pltpu.roll(array(row + 1), HD - off, 1)
    lane = lax.broadcasted_iota(jnp.int32, first.shape, 1)
    return jnp.where(lane < HD - off, low, high)


PEERS = [(dy, dc) for dy in (4, 3, -3, 2, -2, 1, -1) for dc in (0, 1)] + [(0, 1)]
EARLY = 2


def kernel(
    len_ref, cut_hbm, gq_hbm, gk_hbm, q_hbm, k_hbm, v_hbm, g_hbm,
    o_ref, gain_out,
    cut_ref, gq_ref, gk_ref,
    stage, recv, obuf, qh_s, kh_s, soft_s, ds_s, bias, gains, parts,
    gsend, gmid, grecv, psend, precv, asend, brecv, csend, crecv,
    small_sem, stage_sem, send_sem, recv_sem, osend_sem, orecv_sem,
    gsend_sem, gmid_sem, hsend_sem, grecv_sem,
    asend_sem, arecv_sem, bsend_sem, brecv_sem, csend_sem, crecv_sem,
):
    clip = lax.axis_index("clip")
    me = lax.axis_index("seq")
    x, z = lax.div(clip, ZS), lax.rem(clip, ZS)
    g, j = lax.div(me, TILES), lax.rem(me, TILES)
    y, core = lax.div(me, 2), lax.rem(me, 2)
    home = g == x

    def seq_peer(n):
        dy, dc = PEERS[n]
        return lax.rem(y + (dy + 8), 8) * 2 + lax.rem(core + dc, 2)

    def at_x(xx):
        return (xx * ZS + z, me)

    def at_z(zz):
        return (x * ZS + zz, me)

    def remote(src, dst, s_sem, r_sem, to):
        pltpu.make_async_remote_copy(
            src_ref=src, dst_ref=dst, send_sem=s_sem, recv_sem=r_sem,
            device_id=to, device_id_type=MESH,
        ).start()

    def done(ref, sem):
        pltpu.make_async_copy(ref, ref, sem).wait()

    small = [
        pltpu.make_async_copy(a, b, small_sem.at[n])
        for n, (a, b) in enumerate(
            ((gq_hbm, gq_ref), (gk_hbm, gk_ref), (cut_hbm, cut_ref))
        )
    ]
    barrier = pltpu.get_barrier_semaphore()
    others = [(clip, seq_peer(n)) for n in range(SEQ - 1)]
    others += [at_x(lax.rem(x + d, XS)) for d in range(1, XS)]
    others += [at_z(lax.rem(z + d, ZS)) for d in range(1, ZS)]
    for to in others:
        pl.semaphore_signal(barrier, inc=1, device_id=to, device_id_type=MESH)
    for n, ref in enumerate((q_hbm, k_hbm, v_hbm, g_hbm)):
        pltpu.make_async_copy(ref, stage.at[n], stage_sem).start()
    for copy in small:
        copy.start()
    for copy in small:
        copy.wait()

    gsend[...] = jnp.zeros_like(gsend)
    gsend[0:1, 0:SLICE] = gq_ref[...]
    gsend[1:2, 0:SLICE] = gk_ref[...]
    done(stage, stage_sem)
    pl.semaphore_wait(barrier, len(others))

    @pl.when(home)
    def _():
        for d in range(1, XS):
            remote(gsend, gmid, gsend_sem, gmid_sem, at_x(lax.rem(x + d, XS)))

    def send_in(h):
        def source(to):
            to_g, to_j = lax.div(to, TILES), lax.rem(to, TILES)
            return stage.at[
                :, :, pl.ds(pl.multiple_of(to_j * TILE, TILE), TILE),
                pl.ds(pl.multiple_of((to_g * GH + h) * HD, HD), HD),
            ]

        place = recv.at[h, :, pl.ds(me * OWN, OWN)]
        for n in range(SEQ - 1):
            to = seq_peer(n)
            remote(source(to), place, send_sem, recv_sem.at[h], (clip, to))
        pltpu.make_async_copy(source(me), place, recv_sem.at[h]).start()

    def loop(lo, hi, step):
        def run(h, _):
            step(h)
            return 0

        lax.fori_loop(lo, hi, run, 0)

    loop(0, 2, send_in)

    @pl.when(home)
    def _():
        gmid[...] = gsend[...]

    @pl.when(jnp.logical_not(home))
    def _():
        done(gmid, gmid_sem)

    for d in range(1, ZS):
        remote(gmid, grecv.at[z], hsend_sem, grecv_sem, at_z(lax.rem(z + d, ZS)))
    pltpu.make_async_copy(gmid, grecv.at[z], grecv_sem).start()

    loop(2, GH, send_in)

    length = len_ref[0]
    cut_a, cut_b = cut_ref[0, 0], cut_ref[0, 1]
    for tb in range(NBLK):
        rows = BLK * (tb + 1)
        s_at = lax.broadcasted_iota(jnp.int32, (rows, BLK), 0)
        t_at = lax.broadcasted_iota(jnp.int32, (rows, BLK), 1) + tb * BLK
        s_f, t_f = s_at // TILE, t_at // TILE
        s_e = (cut_a <= s_f).astype(jnp.int32) + (cut_b <= s_f).astype(jnp.int32)
        t_e = (cut_a <= t_f).astype(jnp.int32) + (cut_b <= t_f).astype(jnp.int32)
        ok = (s_f <= t_f) & (s_e == t_e) & (t_f < length) & (s_at % TILE == t_at % TILE)
        bias[0:rows, tb * BLK : (tb + 1) * BLK] = jnp.where(ok, 0.0, -1e30)

    done(grecv, grecv_sem)
    gains[...] = jnp.zeros_like(gains)
    for zz in range(ZS):
        row, off = divmod(zz * SLICE, HD)
        for n in range(2):
            piece = grecv[zz, n : n + 1, :]
            moved = pltpu.roll(piece, off, 1) if off else piece
            lane = lax.broadcasted_iota(jnp.int32, (1, HD), 1)
            gains[n, row : row + 1, :] += jnp.where(lane >= off, moved, 0.0)
            if off + SLICE > HD:
                gains[n, row + 1 : row + 2, :] += jnp.where(lane < off + SLICE - HD, moved, 0.0)

    scale = 1.0 / math.sqrt(HD)
    along = (((1,), (1,)), ((), ()))
    down = (((0,), (0,)), ((), ()))
    plain = (((1,), (0,)), ((), ()))

    def dot(a, b, dims):
        return lax.dot_general(a, b, dims, preferred_element_type=F32)

    def mean(a):
        return jnp.sum(a, axis=-1, keepdims=True) * (1.0 / HD)

    def flat(ref, lo, hi):
        return ref[lo // TILE : hi // TILE].reshape(hi - lo, HD)

    def restore(raw, inv, gain, grad, n, h, lo):
        scaled = gain * grad
        normed = raw * inv
        out = inv * (scaled - normed * mean(normed * scaled))
        obuf[h, n, lo // TILE : (lo + BLK) // TILE] = out.astype(BF16).reshape(BF, TILE, HD)
        return jnp.sum(normed * grad, axis=0, keepdims=True)

    def head(h):
        done(recv.at[h], recv_sem.at[h])
        q_r, k_r, v_r, g_r = (recv.at[h, n] for n in range(4))
        gain_q = gains[0, pl.ds(h, 1), :]
        gain_k = gains[1, pl.ds(h, 1), :]
        inv_q, inv_k = [], []
        for b in range(NBLK):
            lo, hi = b * BLK, (b + 1) * BLK
            for src, invs, gain, dst in ((q_r, inv_q, gain_q, qh_s), (k_r, inv_k, gain_k, kh_s)):
                raw = flat(src, lo, hi).astype(F32)
                inv = lax.rsqrt(mean(raw * raw) + EPS)
                invs.append(inv)
                dst[lo:hi] = (raw * inv * gain).astype(BF16)

        part_q = jnp.zeros((1, HD), F32)
        part_k = jnp.zeros((1, HD), F32)
        for b in range(NBLK):
            lo, hi = b * BLK, (b + 1) * BLK
            scores = dot(kh_s[0:hi], qh_s[lo:hi], along)
            exps = jnp.exp(scores * scale + bias[0:hi, lo:hi])
            frame = (lax.broadcasted_iota(jnp.int32, (1, BLK), 1) + lo) // TILE
            dead = (frame >= length).astype(F32)
            total = jnp.sum(exps, axis=0, keepdims=True) + dead
            soft = exps * (1.0 / total)
            soft_b = soft.astype(BF16)
            dprob = dot(flat(v_r, 0, hi), flat(g_r, lo, hi), along)
            delta = jnp.sum(soft_b.astype(F32) * dprob, axis=0, keepdims=True)
            ds_b = (soft * (dprob - delta)).astype(BF16)
            soft_s[0:hi, lo:hi] = soft_b
            ds_s[0:hi, lo:hi] = ds_b
            dq = dot(ds_b, kh_s[0:hi], down) * scale
            raw = flat(q_r, lo, hi).astype(F32)
            part_q += restore(raw, inv_q[b], gain_q, dq, 0, h, lo)
        for b in range(NBLK):
            lo, hi = b * BLK, (b + 1) * BLK
            dk = dot(ds_s[lo:hi, lo:ROWS], qh_s[lo:ROWS], plain) * scale
            raw = flat(k_r, lo, hi).astype(F32)
            part_k += restore(raw, inv_k[b], gain_k, dk, 1, h, lo)
            dv = dot(soft_s[lo:hi, lo:ROWS], flat(g_r, lo, ROWS), plain)
            obuf[h, 2, lo // TILE : hi // TILE] = dv.astype(BF16).reshape(BF, TILE, HD)
        parts[0, pl.ds(h, 1), :] = part_q
        parts[1, pl.ds(h, 1), :] = part_k

        @pl.when(h < EARLY)
        def _():
            send_out(h)

    def send_out(h):
        place = o_ref.at[
            :, :, pl.ds(pl.multiple_of(j * TILE, TILE), TILE),
            pl.ds(pl.multiple_of((g * GH + h) * HD, HD), HD),
        ]
        for n in range(SEQ - 1):
            to = seq_peer(n)
            remote(
                obuf.at[h, :, pl.ds(to * OWN, OWN)], place, osend_sem, orecv_sem, (clip, to)
            )
        pltpu.make_async_copy(obuf.at[h, :, pl.ds(me * OWN, OWN)], place, orecv_sem).start()

    loop(0, GH, head)

    for zz in range(ZS):
        for n in range(2):
            psend[zz, n : n + 1, :] = lanes(lambda r: parts[n, r : r + 1, :], zz * SLICE)
    for d in range(1, ZS):
        zz = lax.rem(z + d, ZS)
        remote(psend.at[zz], precv.at[z], asend_sem, arecv_sem, at_z(zz))
    pltpu.make_async_copy(psend.at[z], precv.at[z], arecv_sem).start()
    send_out(EARLY)
    done(precv, arecv_sem)
    asend[...] = jnp.sum(precv[...], axis=0)

    @pl.when(home)
    def _():
        pltpu.make_async_copy(asend, brecv.at[x], brecv_sem).start()

    @pl.when(jnp.logical_not(home))
    def _():
        remote(asend, brecv.at[x], bsend_sem, brecv_sem, at_x(g))

    send_out(EARLY + 1)

    @pl.when(home)
    def _():
        done(brecv, brecv_sem)
        csend[...] = jnp.sum(brecv[...], axis=0)
        for n in range(SEQ - 1):
            remote(csend, crecv.at[j], csend_sem, crecv_sem, (clip, seq_peer(n)))
        pltpu.make_async_copy(csend, crecv.at[j], crecv_sem).start()

    send_out(EARLY + 2)
    done(crecv.at[pl.ds(0, TILES)], crecv_sem)
    gain_out[...] = jnp.sum(crecv[0:TILES], axis=0)

    @pl.when(home)
    def _():
        done(brecv.at[pl.ds(0, XS - 1)], gsend_sem)
        done(crecv.at[pl.ds(0, SEQ - 1)], csend_sem)

    @pl.when(jnp.logical_not(home))
    def _():
        done(asend, bsend_sem)

    done(grecv.at[pl.ds(0, ZS - 1)], hsend_sem)
    done(precv.at[pl.ds(0, ZS - 1)], asend_sem)
    done(recv.at[:, :, pl.ds(0, FRAMES - OWN)], send_sem)
    done(obuf.at[:, :, pl.ds(0, FRAMES - OWN)], osend_sem)
    done(o_ref, orecv_sem)


def body(queries, key_rows, values, cotangent, lengths, episode_cuts, gain_q, gain_k):
    vmem = pl.BlockSpec(memory_space=pltpu.VMEM)
    hbm = pl.BlockSpec(memory_space=pltpu.HBM)
    dma = pltpu.SemaphoreType.DMA
    width = HEADS * HD
    row = pltpu.VMEM((2, HD), F32)
    out, gain = pl.pallas_call(
        kernel,
        out_shape=(
            pltpu.VMEM((3, OWN, PATCHES, width), BF16),
            pltpu.VMEM((2, HD), F32),
        ),
        in_specs=[pl.BlockSpec(memory_space=pltpu.SMEM)] + [hbm] * 7,
        out_specs=(vmem, vmem),
        scratch_shapes=[
            pltpu.SMEM((1, 2), jnp.int32),
            pltpu.VMEM((1, SLICE), F32),
            pltpu.VMEM((1, SLICE), F32),
            pltpu.VMEM((4, OWN, PATCHES, width), BF16),
            pltpu.VMEM((GH, 4, FRAMES, TILE, HD), BF16),
            pltpu.VMEM((GH, 3, FRAMES, TILE, HD), BF16),
            pltpu.VMEM((ROWS, HD), BF16),
            pltpu.VMEM((ROWS, HD), BF16),
            pltpu.VMEM((ROWS, ROWS), BF16),
            pltpu.VMEM((ROWS, ROWS), BF16),
            pltpu.VMEM((ROWS, ROWS), F32),
            pltpu.VMEM((2, 8, HD), F32),
            pltpu.VMEM((2, 8, HD), F32),
            row,
            row,
            pltpu.VMEM((ZS, 2, HD), F32),
            pltpu.VMEM((ZS, 2, HD), F32),
            pltpu.VMEM((ZS, 2, HD), F32),
            row,
            pltpu.VMEM((XS, 2, HD), F32),
            row,
            pltpu.VMEM((SEQ, 2, HD), F32),
            dma((3,)), dma, dma, dma((GH,)), dma, dma,
            dma, dma, dma, dma,
            dma, dma, dma, dma, dma, dma,
        ],
        compiler_params=pltpu.CompilerParams(
            collective_id=0, has_side_effects=True, vmem_limit_bytes=40 * 2**20
        ),
    )(
        lengths,
        *(
            pltpu.with_memory_space_constraint(a, pltpu.HBM)
            for a in (
                episode_cuts, gain_q.reshape(1, SLICE), gain_k.reshape(1, SLICE),
                *(a.reshape(OWN, PATCHES, width) for a in (queries, key_rows, values, cotangent)),
            )
        )
    )
    return (out[0][None], out[1][None], out[2][None], gain[0, :SLICE], gain[1, :SLICE])


def solution(mesh):
    rows = P("clip", "seq", None, None)
    return jax.shard_map(
        body,
        mesh=mesh,
        in_specs=(rows, rows, rows, rows, P("clip"), P("clip", None), P("clip"), P("clip")),
        out_specs=(rows, rows, rows, P("clip"), P("clip")),
        check_vma=False,
    )
```

```python
import math

import jax
import jax.numpy as jnp
from jax import lax
from jax.experimental import pallas as pl
from jax.experimental.pallas import tpu as pltpu
from jax.sharding import PartitionSpec as P

HEADS = 20
HD = 128
EPS = 1e-06
FRAMES = 32
XS = 4
ZS = 8
SEQ = 16
OWN = FRAMES // SEQ
TILE = 16
PATCHES = 64
TILES = PATCHES // TILE
GROUPS = SEQ // TILES
GH = HEADS // GROUPS
ROWS = FRAMES * TILE
BLK = 128
NBLK = ROWS // BLK
BF = BLK // TILE
SLICE = HEADS * HD // (XS * ZS)
MESH = pl.DeviceIdType.MESH
F32 = jnp.float32
BF16 = jnp.bfloat16


def lanes(array, start):
    row, off = divmod(start, HD)
    first = array(row)
    if off == 0:
        return first
    low = pltpu.roll(first, HD - off, 1)
    if row + 1 >= GH:
        return low
    high = pltpu.roll(array(row + 1), HD - off, 1)
    lane = lax.broadcasted_iota(jnp.int32, first.shape, 1)
    return jnp.where(lane < HD - off, low, high)


PEERS = [(dy, dc) for dy in (4, 3, -3, 2, -2, 1, -1) for dc in (0, 1)] + [(0, 1)]
EARLY = 1


def kernel(
    len_ref, cut_hbm, gq_hbm, gk_hbm, q_hbm, k_hbm, v_hbm, g_hbm,
    o_ref, gain_out,
    cut_ref, gq_ref, gk_ref,
    stage, recv, obuf, qh_s, kh_s, soft_s, ds_s, bias, gains, parts,
    gsend, gmid, grecv, parts_in, psend, precv, asend, brecv, csend, crecv, ready,
    small_sem, stage_sem, send_sem, recv_sem, osend_sem, orecv_sem,
    gsend_sem, gmid_sem, hsend_sem, grecv_sem, pass_sem, pair_sem,
    asend_sem, arecv_sem, bsend_sem, brecv_sem, csend_sem, crecv_sem,
):
    clip = lax.axis_index("clip")
    me = lax.axis_index("seq")
    x, z = lax.div(clip, ZS), lax.rem(clip, ZS)
    g, j = lax.div(me, TILES), lax.rem(me, TILES)
    y, core = lax.div(me, 2), lax.rem(me, 2)
    agent = core == 0
    home = g == x
    inner = jnp.logical_and(agent, home)
    outer = jnp.logical_and(agent, jnp.logical_not(home))
    other = (clip, me + 1 - 2 * core)

    def seq_peer(n):
        dy, dc = PEERS[n]
        return lax.rem(y + (dy + 8), 8) * 2 + lax.rem(core + dc, 2)

    def at_x(xx):
        return (xx * ZS + z, me)

    def at_z(zz):
        return (x * ZS + zz, me)

    def remote(src, dst, s_sem, r_sem, to):
        pltpu.make_async_remote_copy(
            src_ref=src, dst_ref=dst, send_sem=s_sem, recv_sem=r_sem,
            device_id=to, device_id_type=MESH,
        ).start()

    def done(ref, sem):
        pltpu.make_async_copy(ref, ref, sem).wait()

    small = [
        pltpu.make_async_copy(a, b, small_sem.at[n])
        for n, (a, b) in enumerate(
            ((gq_hbm, gq_ref), (gk_hbm, gk_ref), (cut_hbm, cut_ref))
        )
    ]
    barrier = pltpu.get_barrier_semaphore()

    def greet(to):
        pl.semaphore_signal(barrier, inc=1, device_id=to, device_id_type=MESH)

    for dy in (4, 3, -3, 2, -2, 1, -1):
        greet((clip, lax.rem(y + (dy + 8), 8) * 2 + 1))

    @pl.when(agent)
    def _():
        greet(other)
        for d in range(1, XS):
            greet(at_x(lax.rem(x + d, XS)))
        for d in range(1, ZS):
            greet(at_z(lax.rem(z + d, ZS)))

    for n, ref in enumerate((q_hbm, k_hbm, v_hbm, g_hbm)):
        pltpu.make_async_copy(ref, stage.at[n], stage_sem).start()
    for copy in small:
        copy.start()
    for copy in small:
        copy.wait()

    gsend[...] = jnp.zeros_like(gsend)
    gsend[0:1, 0:SLICE] = gq_ref[...]
    gsend[1:2, 0:SLICE] = gk_ref[...]
    parts[...] = jnp.zeros_like(parts)

    @pl.when(core == 1)
    def _():
        pl.semaphore_wait(barrier, SEQ - 1)
        pl.semaphore_signal(ready, inc=1, device_id=other, device_id_type=MESH)

    @pl.when(agent)
    def _():
        pl.semaphore_wait(ready, 1)

    done(stage, stage_sem)

    def send_in(h):
        def source(to):
            to_g, to_j = lax.div(to, TILES), lax.rem(to, TILES)
            return stage.at[
                :, :, pl.ds(pl.multiple_of(to_j * TILE, TILE), TILE),
                pl.ds(pl.multiple_of((to_g * GH + h) * HD, HD), HD),
            ]

        place = recv.at[h, :, pl.ds(me * OWN, OWN)]
        for n in range(SEQ - 1):
            to = seq_peer(n)
            remote(source(to), place, send_sem, recv_sem.at[h], (clip, to))
        pltpu.make_async_copy(source(me), place, recv_sem.at[h]).start()

    def loop(lo, hi, step):
        def run(h, _):
            step(h)
            return 0

        lax.fori_loop(lo, hi, run, 0)

    loop(0, 1, send_in)

    @pl.when(agent)
    def _():
        pl.semaphore_wait(barrier, XS - 1 + ZS - 1)

    @pl.when(inner)
    def _():
        for d in range(1, XS):
            remote(gsend, gmid, gsend_sem, gmid_sem, at_x(lax.rem(x + d, XS)))

    loop(1, 2, send_in)

    @pl.when(inner)
    def _():
        gmid[...] = gsend[...]

    @pl.when(outer)
    def _():
        done(gmid, gmid_sem)

    @pl.when(agent)
    def _():
        for d in range(1, ZS):
            remote(gmid, grecv.at[z], hsend_sem, grecv_sem, at_z(lax.rem(z + d, ZS)))
        pltpu.make_async_copy(gmid, grecv.at[z], grecv_sem).start()

    loop(2, 3, send_in)

    @pl.when(agent)
    def _():
        done(grecv, grecv_sem)
        remote(grecv, grecv, pass_sem, grecv_sem, other)

    loop(3, GH, send_in)

    length = len_ref[0]
    cut_a, cut_b = cut_ref[0, 0], cut_ref[0, 1]
    for tb in range(NBLK):
        rows = BLK * (tb + 1)
        s_at = lax.broadcasted_iota(jnp.int32, (rows, BLK), 0)
        t_at = lax.broadcasted_iota(jnp.int32, (rows, BLK), 1) + tb * BLK
        s_f, t_f = s_at // TILE, t_at // TILE
        s_e = (cut_a <= s_f).astype(jnp.int32) + (cut_b <= s_f).astype(jnp.int32)
        t_e = (cut_a <= t_f).astype(jnp.int32) + (cut_b <= t_f).astype(jnp.int32)
        ok = (s_f <= t_f) & (s_e == t_e) & (t_f < length) & (s_at % TILE == t_at % TILE)
        bias[0:rows, tb * BLK : (tb + 1) * BLK] = jnp.where(ok, 0.0, -1e30)

    @pl.when(core == 1)
    def _():
        done(grecv, grecv_sem)

    gains[...] = jnp.zeros_like(gains)
    for zz in range(ZS):
        row, off = divmod(zz * SLICE, HD)
        for n in range(2):
            piece = grecv[zz, n : n + 1, :]
            moved = pltpu.roll(piece, off, 1) if off else piece
            lane = lax.broadcasted_iota(jnp.int32, (1, HD), 1)
            gains[n, row : row + 1, :] += jnp.where(lane >= off, moved, 0.0)
            if off + SLICE > HD:
                gains[n, row + 1 : row + 2, :] += jnp.where(lane < off + SLICE - HD, moved, 0.0)

    scale = 1.0 / math.sqrt(HD)
    along = (((1,), (1,)), ((), ()))
    down = (((0,), (0,)), ((), ()))
    plain = (((1,), (0,)), ((), ()))

    def dot(a, b, dims):
        return lax.dot_general(a, b, dims, preferred_element_type=F32)

    def mean(a):
        return jnp.sum(a, axis=-1, keepdims=True) * (1.0 / HD)

    def flat(ref, lo, hi):
        return ref[lo // TILE : hi // TILE].reshape(hi - lo, HD)

    def restore(raw, inv, gain, grad, n, h, lo):
        scaled = gain * grad
        normed = raw * inv
        out = inv * (scaled - normed * mean(normed * scaled))
        obuf[h, n, lo // TILE : (lo + BLK) // TILE] = out.astype(BF16).reshape(BF, TILE, HD)
        return jnp.sum(normed * grad, axis=0, keepdims=True)

    def head(h):
        done(recv.at[h], recv_sem.at[h])
        q_r, k_r, v_r, g_r = (recv.at[h, n] for n in range(4))
        gain_q = gains[0, pl.ds(h, 1), :]
        gain_k = gains[1, pl.ds(h, 1), :]
        inv_q, inv_k = [], []
        for b in range(NBLK):
            lo, hi = b * BLK, (b + 1) * BLK
            for src, invs, gain, dst in ((q_r, inv_q, gain_q, qh_s), (k_r, inv_k, gain_k, kh_s)):
                raw = flat(src, lo, hi).astype(F32)
                inv = lax.rsqrt(mean(raw * raw) + EPS)
                invs.append(inv)
                dst[lo:hi] = (raw * inv * gain).astype(BF16)

        part_q = jnp.zeros((1, HD), F32)
        part_k = jnp.zeros((1, HD), F32)
        for b in range(NBLK):
            lo, hi = b * BLK, (b + 1) * BLK
            scores = dot(kh_s[0:hi], qh_s[lo:hi], along)
            exps = jnp.exp(scores * scale + bias[0:hi, lo:hi])
            frame = (lax.broadcasted_iota(jnp.int32, (1, BLK), 1) + lo) // TILE
            dead = (frame >= length).astype(F32)
            total = jnp.sum(exps, axis=0, keepdims=True) + dead
            soft = exps * (1.0 / total)
            soft_b = soft.astype(BF16)
            dprob = dot(flat(v_r, 0, hi), flat(g_r, lo, hi), along)
            delta = jnp.sum(soft_b.astype(F32) * dprob, axis=0, keepdims=True)
            ds_b = (soft * (dprob - delta)).astype(BF16)
            soft_s[0:hi, lo:hi] = soft_b
            ds_s[0:hi, lo:hi] = ds_b
            dq = dot(ds_b, kh_s[0:hi], down) * scale
            raw = flat(q_r, lo, hi).astype(F32)
            part_q += restore(raw, inv_q[b], gain_q, dq, 0, h, lo)
        for b in range(NBLK):
            lo, hi = b * BLK, (b + 1) * BLK
            dk = dot(ds_s[lo:hi, lo:ROWS], qh_s[lo:ROWS], plain) * scale
            raw = flat(k_r, lo, hi).astype(F32)
            part_k += restore(raw, inv_k[b], gain_k, dk, 1, h, lo)
            dv = dot(soft_s[lo:hi, lo:ROWS], flat(g_r, lo, ROWS), plain)
            obuf[h, 2, lo // TILE : hi // TILE] = dv.astype(BF16).reshape(BF, TILE, HD)
        parts[0, pl.ds(h, 1), :] = part_q
        parts[1, pl.ds(h, 1), :] = part_k

        @pl.when(h < EARLY)
        def _():
            send_out(h)

    def send_out(h):
        place = o_ref.at[
            :, :, pl.ds(pl.multiple_of(j * TILE, TILE), TILE),
            pl.ds(pl.multiple_of((g * GH + h) * HD, HD), HD),
        ]
        for n in range(SEQ - 1):
            to = seq_peer(n)
            remote(
                obuf.at[h, :, pl.ds(to * OWN, OWN)], place, osend_sem, orecv_sem, (clip, to)
            )
        pltpu.make_async_copy(obuf.at[h, :, pl.ds(me * OWN, OWN)], place, orecv_sem).start()

    loop(0, GH, head)

    @pl.when(core == 1)
    def _():
        remote(parts, parts_in, pass_sem, pair_sem, other)

    send_out(EARLY)

    @pl.when(agent)
    def _():
        done(parts_in, pair_sem)
        parts[...] += parts_in[...]
        for zz in range(ZS):
            for n in range(2):
                psend[zz, n : n + 1, :] = lanes(lambda r: parts[n, r : r + 1, :], zz * SLICE)
        for d in range(1, ZS):
            zz = lax.rem(z + d, ZS)
            remote(psend.at[zz], precv.at[z], asend_sem, arecv_sem, at_z(zz))
        pltpu.make_async_copy(psend.at[z], precv.at[z], arecv_sem).start()

    send_out(EARLY + 1)

    @pl.when(agent)
    def _():
        done(precv, arecv_sem)
        asend[...] = jnp.sum(precv[...], axis=0)

    @pl.when(inner)
    def _():
        pltpu.make_async_copy(asend, brecv.at[x], brecv_sem).start()

    @pl.when(outer)
    def _():
        remote(asend, brecv.at[x], bsend_sem, brecv_sem, at_x(g))

    send_out(EARLY + 2)

    @pl.when(inner)
    def _():
        done(brecv, brecv_sem)
        csend[...] = jnp.sum(brecv[...], axis=0)
        slot = lax.div(j, 2)
        for n in range(SEQ - 1):
            remote(csend, crecv.at[slot], csend_sem, crecv_sem, (clip, seq_peer(n)))
        pltpu.make_async_copy(csend, crecv.at[slot], crecv_sem).start()

    send_out(EARLY + 3)
    done(crecv.at[pl.ds(0, 2)], crecv_sem)
    gain_out[...] = crecv[0] + crecv[1]

    @pl.when(inner)
    def _():
        done(brecv.at[pl.ds(0, XS - 1)], gsend_sem)
        done(crecv.at[pl.ds(0, SEQ - 1)], csend_sem)

    @pl.when(outer)
    def _():
        done(asend, bsend_sem)

    @pl.when(agent)
    def _():
        done(grecv.at[pl.ds(0, ZS - 1)], hsend_sem)
        done(precv.at[pl.ds(0, ZS - 1)], asend_sem)
        done(grecv, pass_sem)

    @pl.when(core == 1)
    def _():
        done(parts_in, pass_sem)

    done(recv.at[:, :, pl.ds(0, FRAMES - OWN)], send_sem)
    done(obuf.at[:, :, pl.ds(0, FRAMES - OWN)], osend_sem)
    done(o_ref, orecv_sem)


def body(queries, key_rows, values, cotangent, lengths, episode_cuts, gain_q, gain_k):
    vmem = pl.BlockSpec(memory_space=pltpu.VMEM)
    hbm = pl.BlockSpec(memory_space=pltpu.HBM)
    dma = pltpu.SemaphoreType.DMA
    width = HEADS * HD
    row = pltpu.VMEM((2, HD), F32)
    out, gain = pl.pallas_call(
        kernel,
        out_shape=(
            pltpu.VMEM((3, OWN, PATCHES, width), BF16),
            pltpu.VMEM((2, HD), F32),
        ),
        in_specs=[pl.BlockSpec(memory_space=pltpu.SMEM)] + [hbm] * 7,
        out_specs=(vmem, vmem),
        scratch_shapes=[
            pltpu.SMEM((1, 2), jnp.int32),
            pltpu.VMEM((1, SLICE), F32),
            pltpu.VMEM((1, SLICE), F32),
            pltpu.VMEM((4, OWN, PATCHES, width), BF16),
            pltpu.VMEM((GH, 4, FRAMES, TILE, HD), BF16),
            pltpu.VMEM((GH, 3, FRAMES, TILE, HD), BF16),
            pltpu.VMEM((ROWS, HD), BF16),
            pltpu.VMEM((ROWS, HD), BF16),
            pltpu.VMEM((ROWS, ROWS), BF16),
            pltpu.VMEM((ROWS, ROWS), BF16),
            pltpu.VMEM((ROWS, ROWS), F32),
            pltpu.VMEM((2, 8, HD), F32),
            pltpu.VMEM((2, 8, HD), F32),
            row,
            row,
            pltpu.VMEM((ZS, 2, HD), F32),
            pltpu.VMEM((2, 8, HD), F32),
            pltpu.VMEM((ZS, 2, HD), F32),
            pltpu.VMEM((ZS, 2, HD), F32),
            row,
            pltpu.VMEM((XS, 2, HD), F32),
            row,
            pltpu.VMEM((SEQ, 2, HD), F32),
            pltpu.SemaphoreType.REGULAR,
            dma((3,)), dma, dma, dma((GH,)), dma, dma,
            dma, dma, dma, dma, dma, dma,
            dma, dma, dma, dma, dma, dma,
        ],
        compiler_params=pltpu.CompilerParams(
            collective_id=0, has_side_effects=True, vmem_limit_bytes=40 * 2**20
        ),
    )(
        lengths,
        *(
            pltpu.with_memory_space_constraint(a, pltpu.HBM)
            for a in (
                episode_cuts, gain_q.reshape(1, SLICE), gain_k.reshape(1, SLICE),
                *(a.reshape(OWN, PATCHES, width) for a in (queries, key_rows, values, cotangent)),
            )
        )
    )
    return (out[0][None], out[1][None], out[2][None], gain[0, :SLICE], gain[1, :SLICE])


def solution(mesh):
    rows = P("clip", "seq", None, None)
    return jax.shard_map(
        body,
        mesh=mesh,
        in_specs=(rows, rows, rows, rows, P("clip"), P("clip", None), P("clip"), P("clip")),
        out_specs=(rows, rows, rows, P("clip"), P("clip")),
        check_vma=False,
    )
```

```python
import math

import jax
import jax.numpy as jnp
from jax import lax
from jax.experimental import pallas as pl
from jax.experimental.pallas import tpu as pltpu
from jax.sharding import PartitionSpec as P

HEADS = 20
HD = 128
EPS = 1e-06
FRAMES = 32
XS = 4
ZS = 8
SEQ = 16
OWN = FRAMES // SEQ
TILE = 16
PATCHES = 64
TILES = PATCHES // TILE
GROUPS = SEQ // TILES
GH = HEADS // GROUPS
ROWS = FRAMES * TILE
BLK = 128
NBLK = ROWS // BLK
BF = BLK // TILE
SLICE = HEADS * HD // (XS * ZS)
MESH = pl.DeviceIdType.MESH
F32 = jnp.float32
BF16 = jnp.bfloat16


def lanes(array, start):
    row, off = divmod(start, HD)
    first = array(row)
    if off == 0:
        return first
    low = pltpu.roll(first, HD - off, 1)
    if row + 1 >= GH:
        return low
    high = pltpu.roll(array(row + 1), HD - off, 1)
    lane = lax.broadcasted_iota(jnp.int32, first.shape, 1)
    return jnp.where(lane < HD - off, low, high)


PEERS = [(dy, dc) for dy in (4, 3, -3, 2, -2, 1, -1) for dc in (0, 1)] + [(0, 1)]
ALIKE = [n for n, (_, dc) in enumerate(PEERS) if dc == 0]
UNLIKE = [n for n, (_, dc) in enumerate(PEERS) if dc == 1]
EARLY = 1


def kernel(
    len_ref, cut_hbm, gq_hbm, gk_hbm, q_hbm, k_hbm, v_hbm, g_hbm,
    o_ref, gain_out,
    cut_ref, gq_ref, gk_ref,
    stage, recv, obuf, qh_s, kh_s, soft_s, ds_s, bias, gains, parts,
    gsend, gmid, grecv, parts_in, psend, precv, asend, brecv, csend, crecv, ready,
    small_sem, stage_sem, send_sem, recv_sem, osend_sem, orecv_sem,
    gsend_sem, gmid_sem, hsend_sem, grecv_sem, pass_sem, pair_sem,
    asend_sem, arecv_sem, bsend_sem, brecv_sem, csend_sem, crecv_sem,
):
    clip = lax.axis_index("clip")
    me = lax.axis_index("seq")
    x, z = lax.div(clip, ZS), lax.rem(clip, ZS)
    g, j = lax.div(me, TILES), lax.rem(me, TILES)
    y, core = lax.div(me, 2), lax.rem(me, 2)
    agent = j == 0
    home = g == x
    inner = jnp.logical_and(agent, home)
    outer = jnp.logical_and(agent, jnp.logical_not(home))

    def seq_peer(n):
        dy, dc = PEERS[n]
        return lax.rem(y + (dy + 8), 8) * 2 + lax.rem(core + dc, 2)

    def at_x(xx):
        return (xx * ZS + z, me)

    def at_z(zz):
        return (x * ZS + zz, me)

    def remote(src, dst, s_sem, r_sem, to):
        pltpu.make_async_remote_copy(
            src_ref=src, dst_ref=dst, send_sem=s_sem, recv_sem=r_sem,
            device_id=to, device_id_type=MESH,
        ).start()

    def done(ref, sem):
        pltpu.make_async_copy(ref, ref, sem).wait()

    small = [
        pltpu.make_async_copy(a, b, small_sem.at[n])
        for n, (a, b) in enumerate(
            ((gq_hbm, gq_ref), (gk_hbm, gk_ref), (cut_hbm, cut_ref))
        )
    ]
    barrier = pltpu.get_barrier_semaphore()

    def greet(to):
        pl.semaphore_signal(barrier, inc=1, device_id=to, device_id_type=MESH)

    def tell(to):
        pl.semaphore_signal(ready, inc=1, device_id=(clip, to), device_id_type=MESH)

    @pl.when(core == 1)
    def _():
        for dy in (4, 3, -3, 2, -2, 1, -1):
            greet((clip, lax.rem(y + (dy + 8), 8) * 2 + 1))

    @pl.when(j == 3)
    def _():
        greet((clip, me - 1))

    @pl.when(core == 0)
    def _():
        for dg in (2, 1, 3):
            greet((clip, lax.rem(g + dg, GROUPS) * TILES + 2))

    @pl.when(agent)
    def _():
        greet((clip, me + 2))
        for d in range(1, XS):
            greet(at_x(lax.rem(x + d, XS)))
        for d in range(1, ZS):
            greet(at_z(lax.rem(z + d, ZS)))

    for n, ref in enumerate((q_hbm, k_hbm, v_hbm, g_hbm)):
        pltpu.make_async_copy(ref, stage.at[n], stage_sem).start()
    for copy in small:
        copy.start()

    def send_to(h, peers):
        def source(to):
            to_g, to_j = lax.div(to, TILES), lax.rem(to, TILES)
            return stage.at[
                :, :, pl.ds(pl.multiple_of(to_j * TILE, TILE), TILE),
                pl.ds(pl.multiple_of((to_g * GH + h) * HD, HD), HD),
            ]

        place = recv.at[h, :, pl.ds(me * OWN, OWN)]
        for n in peers:
            to = seq_peer(n)
            remote(source(to), place, send_sem, recv_sem.at[h], (clip, to))
        return source(me), place

    def send_in(h):
        mine, place = send_to(h, range(SEQ - 1))
        pltpu.make_async_copy(mine, place, recv_sem.at[h]).start()

    def send_alike(h):
        send_to(h, ALIKE)

    def send_unlike(h):
        mine, place = send_to(h, UNLIKE)
        pltpu.make_async_copy(mine, place, recv_sem.at[h]).start()

    def loop(lo, hi, step):
        def run(h, _):
            step(h)
            return 0

        lax.fori_loop(lo, hi, run, 0)

    @pl.when(j == 2)
    def _():
        pl.semaphore_wait(barrier, SEQ // 2)
        tell(me + 1)

    @pl.when(core == 1)
    def _():
        pl.semaphore_wait(barrier, SEQ // 2 - 1)
        done(stage, stage_sem)
        loop(0, 2, send_alike)

    pl.semaphore_wait(ready, 1)

    @pl.when(j == 3)
    def _():
        for d in (3, 2, 1):
            tell(me - d)

    @pl.when(core == 0)
    def _():
        done(stage, stage_sem)
        loop(0, 1, send_alike)

    loop(0, 1, send_unlike)
    for copy in small:
        copy.wait()
    gsend[...] = jnp.zeros_like(gsend)
    gsend[0:1, 0:SLICE] = gq_ref[...]
    gsend[1:2, 0:SLICE] = gk_ref[...]
    parts[...] = jnp.zeros_like(parts)

    @pl.when(agent)
    def _():
        pl.semaphore_wait(barrier, XS - 1 + ZS - 1)

    @pl.when(inner)
    def _():
        for d in range(1, XS):
            remote(gsend, gmid, gsend_sem, gmid_sem, at_x(lax.rem(x + d, XS)))

    @pl.when(core == 0)
    def _():
        loop(1, 2, send_alike)

    loop(1, 2, send_unlike)

    @pl.when(inner)
    def _():
        gmid[...] = gsend[...]

    @pl.when(outer)
    def _():
        done(gmid, gmid_sem)

    @pl.when(agent)
    def _():
        for d in range(1, ZS):
            remote(gmid, grecv.at[z], hsend_sem, grecv_sem, at_z(lax.rem(z + d, ZS)))
        pltpu.make_async_copy(gmid, grecv.at[z], grecv_sem).start()

    loop(2, 3, send_in)

    @pl.when(agent)
    def _():
        done(grecv, grecv_sem)
        for d in range(1, TILES):
            remote(grecv, grecv, pass_sem, grecv_sem, (clip, me + d))

    loop(3, GH, send_in)

    length = len_ref[0]
    cut_a, cut_b = cut_ref[0, 0], cut_ref[0, 1]
    for tb in range(NBLK):
        rows = BLK * (tb + 1)
        s_at = lax.broadcasted_iota(jnp.int32, (rows, BLK), 0)
        t_at = lax.broadcasted_iota(jnp.int32, (rows, BLK), 1) + tb * BLK
        s_f, t_f = s_at // TILE, t_at // TILE
        s_e = (cut_a <= s_f).astype(jnp.int32) + (cut_b <= s_f).astype(jnp.int32)
        t_e = (cut_a <= t_f).astype(jnp.int32) + (cut_b <= t_f).astype(jnp.int32)
        ok = (s_f <= t_f) & (s_e == t_e) & (t_f < length) & (s_at % TILE == t_at % TILE)
        bias[0:rows, tb * BLK : (tb + 1) * BLK] = jnp.where(ok, 0.0, -1e30)

    @pl.when(jnp.logical_not(agent))
    def _():
        done(grecv, grecv_sem)

    gains[...] = jnp.zeros_like(gains)
    for zz in range(ZS):
        row, off = divmod(zz * SLICE, HD)
        for n in range(2):
            piece = grecv[zz, n : n + 1, :]
            moved = pltpu.roll(piece, off, 1) if off else piece
            lane = lax.broadcasted_iota(jnp.int32, (1, HD), 1)
            gains[n, row : row + 1, :] += jnp.where(lane >= off, moved, 0.0)
            if off + SLICE > HD:
                gains[n, row + 1 : row + 2, :] += jnp.where(lane < off + SLICE - HD, moved, 0.0)

    scale = 1.0 / math.sqrt(HD)
    along = (((1,), (1,)), ((), ()))
    down = (((0,), (0,)), ((), ()))
    plain = (((1,), (0,)), ((), ()))

    def dot(a, b, dims):
        return lax.dot_general(a, b, dims, preferred_element_type=F32)

    def mean(a):
        return jnp.sum(a, axis=-1, keepdims=True) * (1.0 / HD)

    def flat(ref, lo, hi):
        return ref[lo // TILE : hi // TILE].reshape(hi - lo, HD)

    def restore(raw, inv, gain, grad, n, h, lo):
        scaled = gain * grad
        normed = raw * inv
        out = inv * (scaled - normed * mean(normed * scaled))
        obuf[h, n, lo // TILE : (lo + BLK) // TILE] = out.astype(BF16).reshape(BF, TILE, HD)
        return jnp.sum(normed * grad, axis=0, keepdims=True)

    def head(h):
        done(recv.at[h], recv_sem.at[h])
        q_r, k_r, v_r, g_r = (recv.at[h, n] for n in range(4))
        gain_q = gains[0, pl.ds(h, 1), :]
        gain_k = gains[1, pl.ds(h, 1), :]
        inv_q, inv_k = [], []
        for b in range(NBLK):
            lo, hi = b * BLK, (b + 1) * BLK
            for src, invs, gain, dst in ((q_r, inv_q, gain_q, qh_s), (k_r, inv_k, gain_k, kh_s)):
                raw = flat(src, lo, hi).astype(F32)
                inv = lax.rsqrt(mean(raw * raw) + EPS)
                invs.append(inv)
                dst[lo:hi] = (raw * inv * gain).astype(BF16)

        part_q = jnp.zeros((1, HD), F32)
        part_k = jnp.zeros((1, HD), F32)
        for b in range(NBLK):
            lo, hi = b * BLK, (b + 1) * BLK
            scores = dot(kh_s[0:hi], qh_s[lo:hi], along)
            exps = jnp.exp(scores * scale + bias[0:hi, lo:hi])
            frame = (lax.broadcasted_iota(jnp.int32, (1, BLK), 1) + lo) // TILE
            dead = (frame >= length).astype(F32)
            total = jnp.sum(exps, axis=0, keepdims=True) + dead
            soft = exps * (1.0 / total)
            soft_b = soft.astype(BF16)
            dprob = dot(flat(v_r, 0, hi), flat(g_r, lo, hi), along)
            delta = jnp.sum(soft_b.astype(F32) * dprob, axis=0, keepdims=True)
            ds_b = (soft * (dprob - delta)).astype(BF16)
            soft_s[0:hi, lo:hi] = soft_b
            ds_s[0:hi, lo:hi] = ds_b
            dq = dot(ds_b, kh_s[0:hi], down) * scale
            raw = flat(q_r, lo, hi).astype(F32)
            part_q += restore(raw, inv_q[b], gain_q, dq, 0, h, lo)
        for b in range(NBLK):
            lo, hi = b * BLK, (b + 1) * BLK
            dk = dot(ds_s[lo:hi, lo:ROWS], qh_s[lo:ROWS], plain) * scale
            raw = flat(k_r, lo, hi).astype(F32)
            part_k += restore(raw, inv_k[b], gain_k, dk, 1, h, lo)
            dv = dot(soft_s[lo:hi, lo:ROWS], flat(g_r, lo, ROWS), plain)
            obuf[h, 2, lo // TILE : hi // TILE] = dv.astype(BF16).reshape(BF, TILE, HD)
        parts[0, pl.ds(h, 1), :] = part_q
        parts[1, pl.ds(h, 1), :] = part_k

        @pl.when(h < EARLY)
        def _():
            send_out(h)

    def send_out(h):
        place = o_ref.at[
            :, :, pl.ds(pl.multiple_of(j * TILE, TILE), TILE),
            pl.ds(pl.multiple_of((g * GH + h) * HD, HD), HD),
        ]
        for n in range(SEQ - 1):
            to = seq_peer(n)
            remote(
                obuf.at[h, :, pl.ds(to * OWN, OWN)], place, osend_sem, orecv_sem, (clip, to)
            )
        pltpu.make_async_copy(obuf.at[h, :, pl.ds(me * OWN, OWN)], place, orecv_sem).start()

    loop(0, GH, head)

    @pl.when(jnp.logical_not(agent))
    def _():
        remote(parts, parts_in.at[j - 1], pass_sem, pair_sem, (clip, me - j))

    send_out(EARLY)

    @pl.when(agent)
    def _():
        done(parts_in, pair_sem)
        parts[...] += jnp.sum(parts_in[...], axis=0)
        for zz in range(ZS):
            for n in range(2):
                psend[zz, n : n + 1, :] = lanes(lambda r: parts[n, r : r + 1, :], zz * SLICE)
        for d in range(1, ZS):
            zz = lax.rem(z + d, ZS)
            remote(psend.at[zz], precv.at[z], asend_sem, arecv_sem, at_z(zz))
        pltpu.make_async_copy(psend.at[z], precv.at[z], arecv_sem).start()

    send_out(EARLY + 1)

    @pl.when(agent)
    def _():
        done(precv, arecv_sem)
        asend[...] = jnp.sum(precv[...], axis=0)

    @pl.when(inner)
    def _():
        pltpu.make_async_copy(asend, brecv.at[x], brecv_sem).start()

    @pl.when(outer)
    def _():
        remote(asend, brecv.at[x], bsend_sem, brecv_sem, at_x(g))

    send_out(EARLY + 2)

    @pl.when(inner)
    def _():
        done(brecv, brecv_sem)
        csend[...] = jnp.sum(brecv[...], axis=0)
        for n in range(SEQ - 1):
            remote(csend, crecv.at[0], csend_sem, crecv_sem, (clip, seq_peer(n)))
        pltpu.make_async_copy(csend, crecv.at[0], crecv_sem).start()

    send_out(EARLY + 3)
    done(crecv.at[0], crecv_sem)
    gain_out[...] = crecv[0]

    @pl.when(inner)
    def _():
        done(brecv.at[pl.ds(0, XS - 1)], gsend_sem)
        done(crecv.at[pl.ds(0, SEQ - 1)], csend_sem)

    @pl.when(outer)
    def _():
        done(asend, bsend_sem)

    @pl.when(agent)
    def _():
        done(grecv.at[pl.ds(0, ZS - 1)], hsend_sem)
        done(precv.at[pl.ds(0, ZS - 1)], asend_sem)
        done(parts_in, pass_sem)

    @pl.when(jnp.logical_not(agent))
    def _():
        done(parts_in.at[0], pass_sem)

    done(recv.at[:, :, pl.ds(0, FRAMES - OWN)], send_sem)
    done(obuf.at[:, :, pl.ds(0, FRAMES - OWN)], osend_sem)
    done(o_ref, orecv_sem)


def body(queries, key_rows, values, cotangent, lengths, episode_cuts, gain_q, gain_k):
    vmem = pl.BlockSpec(memory_space=pltpu.VMEM)
    hbm = pl.BlockSpec(memory_space=pltpu.HBM)
    dma = pltpu.SemaphoreType.DMA
    width = HEADS * HD
    row = pltpu.VMEM((2, HD), F32)
    out, gain = pl.pallas_call(
        kernel,
        out_shape=(
            pltpu.VMEM((3, OWN, PATCHES, width), BF16),
            pltpu.VMEM((2, HD), F32),
        ),
        in_specs=[pl.BlockSpec(memory_space=pltpu.SMEM)] + [hbm] * 7,
        out_specs=(vmem, vmem),
        scratch_shapes=[
            pltpu.SMEM((1, 2), jnp.int32),
            pltpu.VMEM((1, SLICE), F32),
            pltpu.VMEM((1, SLICE), F32),
            pltpu.VMEM((4, OWN, PATCHES, width), BF16),
            pltpu.VMEM((GH, 4, FRAMES, TILE, HD), BF16),
            pltpu.VMEM((GH, 3, FRAMES, TILE, HD), BF16),
            pltpu.VMEM((ROWS, HD), BF16),
            pltpu.VMEM((ROWS, HD), BF16),
            pltpu.VMEM((ROWS, ROWS), BF16),
            pltpu.VMEM((ROWS, ROWS), BF16),
            pltpu.VMEM((ROWS, ROWS), F32),
            pltpu.VMEM((2, 8, HD), F32),
            pltpu.VMEM((2, 8, HD), F32),
            row,
            row,
            pltpu.VMEM((ZS, 2, HD), F32),
            pltpu.VMEM((TILES - 1, 2, 8, HD), F32),
            pltpu.VMEM((ZS, 2, HD), F32),
            pltpu.VMEM((ZS, 2, HD), F32),
            row,
            pltpu.VMEM((XS, 2, HD), F32),
            row,
            pltpu.VMEM((SEQ, 2, HD), F32),
            pltpu.SemaphoreType.REGULAR,
            dma((3,)), dma, dma, dma((GH,)), dma, dma,
            dma, dma, dma, dma, dma, dma,
            dma, dma, dma, dma, dma, dma,
        ],
        compiler_params=pltpu.CompilerParams(
            collective_id=0, has_side_effects=True, vmem_limit_bytes=40 * 2**20
        ),
    )(
        lengths,
        *(
            pltpu.with_memory_space_constraint(a, pltpu.HBM)
            for a in (
                episode_cuts, gain_q.reshape(1, SLICE), gain_k.reshape(1, SLICE),
                *(a.reshape(OWN, PATCHES, width) for a in (queries, key_rows, values, cotangent)),
            )
        )
    )
    return (out[0][None], out[1][None], out[2][None], gain[0, :SLICE], gain[1, :SLICE])


def solution(mesh):
    rows = P("clip", "seq", None, None)
    return jax.shard_map(
        body,
        mesh=mesh,
        in_specs=(rows, rows, rows, rows, P("clip"), P("clip", None), P("clip"), P("clip")),
        out_specs=(rows, rows, rows, P("clip"), P("clip")),
        check_vma=False,
    )
```

```python
import math

import jax
import jax.numpy as jnp
from jax import lax
from jax.experimental import pallas as pl
from jax.experimental.pallas import tpu as pltpu
from jax.sharding import PartitionSpec as P

HEADS = 20
HD = 128
EPS = 1e-06
FRAMES = 32
XS = 4
ZS = 8
SEQ = 16
OWN = FRAMES // SEQ
TILE = 16
PATCHES = 64
TILES = PATCHES // TILE
GROUPS = SEQ // TILES
GH = HEADS // GROUPS
ROWS = FRAMES * TILE
BLK = 128
NBLK = ROWS // BLK
BF = BLK // TILE
SLICE = HEADS * HD // (XS * ZS)
MESH = pl.DeviceIdType.MESH
F32 = jnp.float32
BF16 = jnp.bfloat16


def lanes(array, start):
    row, off = divmod(start, HD)
    first = array(row)
    if off == 0:
        return first
    low = pltpu.roll(first, HD - off, 1)
    if row + 1 >= GH:
        return low
    high = pltpu.roll(array(row + 1), HD - off, 1)
    lane = lax.broadcasted_iota(jnp.int32, first.shape, 1)
    return jnp.where(lane < HD - off, low, high)


PEERS = [(dy, dc) for dy in (4, 3, -3, 2, -2, 1, -1) for dc in (0, 1)] + [(0, 1)]
ALIKE = [n for n, (_, dc) in enumerate(PEERS) if dc == 0]
UNLIKE = [n for n, (_, dc) in enumerate(PEERS) if dc == 1]
EARLY = 1


def kernel(
    len_ref, cut_hbm, gq_hbm, gk_hbm, q_hbm, k_hbm, v_hbm, g_hbm,
    o_ref, gain_out,
    cut_ref, gq_ref, gk_ref,
    stage, recv, obuf, qh_s, kh_s, soft_s, ds_s, bias, gains, parts,
    gsend, gmid, grecv, parts_in, psend, precv, asend, brecv, csend, crecv, ready,
    small_sem, stage_sem, send_sem, recv_sem, osend_sem, orecv_sem,
    gsend_sem, gmid_sem, hsend_sem, grecv_sem, pass_sem, pair_sem,
    asend_sem, arecv_sem, bsend_sem, brecv_sem, csend_sem, crecv_sem,
):
    clip = lax.axis_index("clip")
    me = lax.axis_index("seq")
    x, z = lax.div(clip, ZS), lax.rem(clip, ZS)
    g, j = lax.div(me, TILES), lax.rem(me, TILES)
    y, core = lax.div(me, 2), lax.rem(me, 2)
    agent = j == 0
    home = g == x
    way = 1 - 2 * core
    inner = jnp.logical_and(agent, home)
    outer = jnp.logical_and(agent, jnp.logical_not(home))

    def seq_peer(n):
        dy, dc = PEERS[n]
        return lax.rem(y + 8 + dy * way, 8) * 2 + lax.rem(core + dc, 2)

    def at_x(xx):
        return (xx * ZS + z, me)

    def at_z(zz):
        return (x * ZS + zz, me)

    def remote(src, dst, s_sem, r_sem, to):
        pltpu.make_async_remote_copy(
            src_ref=src, dst_ref=dst, send_sem=s_sem, recv_sem=r_sem,
            device_id=to, device_id_type=MESH,
        ).start()

    def done(ref, sem):
        pltpu.make_async_copy(ref, ref, sem).wait()

    small = [
        pltpu.make_async_copy(a, b, small_sem.at[n])
        for n, (a, b) in enumerate(
            ((gq_hbm, gq_ref), (gk_hbm, gk_ref), (cut_hbm, cut_ref))
        )
    ]
    barrier = pltpu.get_barrier_semaphore()

    def greet(to):
        pl.semaphore_signal(barrier, inc=1, device_id=to, device_id_type=MESH)

    def tell(to):
        pl.semaphore_signal(ready, inc=1, device_id=(clip, to), device_id_type=MESH)

    @pl.when(core == 1)
    def _():
        for dy in (4, 3, -3, 2, -2, 1, -1):
            greet((clip, lax.rem(y + (dy + 8), 8) * 2 + 1))

    @pl.when(j == 3)
    def _():
        greet((clip, me - 1))

    @pl.when(core == 0)
    def _():
        for dg in (2, 1, 3):
            greet((clip, lax.rem(g + dg, GROUPS) * TILES + 2))

    @pl.when(agent)
    def _():
        greet((clip, me + 2))
        for d in range(1, XS):
            greet(at_x(lax.rem(x + d, XS)))
        for d in range(1, ZS):
            greet(at_z(lax.rem(z + d, ZS)))

    for n, ref in enumerate((q_hbm, k_hbm, v_hbm, g_hbm)):
        pltpu.make_async_copy(ref, stage.at[n], stage_sem).start()
    for copy in small:
        copy.start()

    def send_to(h, peers):
        def source(to):
            to_g, to_j = lax.div(to, TILES), lax.rem(to, TILES)
            return stage.at[
                :, :, pl.ds(pl.multiple_of(to_j * TILE, TILE), TILE),
                pl.ds(pl.multiple_of((to_g * GH + h) * HD, HD), HD),
            ]

        place = recv.at[h, :, pl.ds(me * OWN, OWN)]
        for n in peers:
            to = seq_peer(n)
            remote(source(to), place, send_sem, recv_sem.at[h], (clip, to))
        return source(me), place

    def send_in(h):
        mine, place = send_to(h, range(SEQ - 1))
        pltpu.make_async_copy(mine, place, recv_sem.at[h]).start()

    def send_alike(h):
        send_to(h, ALIKE)

    def send_unlike(h):
        mine, place = send_to(h, UNLIKE)
        pltpu.make_async_copy(mine, place, recv_sem.at[h]).start()

    def loop(lo, hi, step):
        def run(h, _):
            step(h)
            return 0

        lax.fori_loop(lo, hi, run, 0)

    @pl.when(j == 2)
    def _():
        pl.semaphore_wait(barrier, SEQ // 2)
        tell(me + 1)

    @pl.when(core == 1)
    def _():
        pl.semaphore_wait(barrier, SEQ // 2 - 1)
        done(stage, stage_sem)
        loop(0, 2, send_alike)

    pl.semaphore_wait(ready, 1)

    @pl.when(j == 3)
    def _():
        for d in (3, 2, 1):
            tell(me - d)

    @pl.when(core == 0)
    def _():
        done(stage, stage_sem)
        loop(0, 1, send_alike)

    loop(0, 1, send_unlike)
    for copy in small:
        copy.wait()
    gsend[...] = jnp.zeros_like(gsend)
    gsend[0:1, 0:SLICE] = gq_ref[...]
    gsend[1:2, 0:SLICE] = gk_ref[...]
    parts[...] = jnp.zeros_like(parts)

    @pl.when(agent)
    def _():
        pl.semaphore_wait(barrier, XS - 1 + ZS - 1)

    @pl.when(inner)
    def _():
        for d in range(1, XS):
            remote(gsend, gmid, gsend_sem, gmid_sem, at_x(lax.rem(x + d, XS)))

    @pl.when(core == 0)
    def _():
        loop(1, 2, send_alike)

    loop(1, 2, send_unlike)

    @pl.when(inner)
    def _():
        gmid[...] = gsend[...]

    @pl.when(outer)
    def _():
        done(gmid, gmid_sem)

    @pl.when(agent)
    def _():
        for d in range(1, ZS):
            remote(gmid, grecv.at[z], hsend_sem, grecv_sem, at_z(lax.rem(z + d, ZS)))
        pltpu.make_async_copy(gmid, grecv.at[z], grecv_sem).start()

    loop(2, 3, send_in)

    @pl.when(agent)
    def _():
        done(grecv, grecv_sem)
        for d in range(1, TILES):
            remote(grecv, grecv, pass_sem, grecv_sem, (clip, me + d))

    loop(3, GH, send_in)

    length = len_ref[0]
    cut_a, cut_b = cut_ref[0, 0], cut_ref[0, 1]
    for tb in range(NBLK):
        rows = BLK * (tb + 1)
        s_at = lax.broadcasted_iota(jnp.int32, (rows, BLK), 0)
        t_at = lax.broadcasted_iota(jnp.int32, (rows, BLK), 1) + tb * BLK
        s_f, t_f = s_at // TILE, t_at // TILE
        s_e = (cut_a <= s_f).astype(jnp.int32) + (cut_b <= s_f).astype(jnp.int32)
        t_e = (cut_a <= t_f).astype(jnp.int32) + (cut_b <= t_f).astype(jnp.int32)
        ok = (s_f <= t_f) & (s_e == t_e) & (t_f < length) & (s_at % TILE == t_at % TILE)
        bias[0:rows, tb * BLK : (tb + 1) * BLK] = jnp.where(ok, 0.0, -1e30)

    @pl.when(jnp.logical_not(agent))
    def _():
        done(grecv, grecv_sem)

    gains[...] = jnp.zeros_like(gains)
    for zz in range(ZS):
        row, off = divmod(zz * SLICE, HD)
        for n in range(2):
            piece = grecv[zz, n : n + 1, :]
            moved = pltpu.roll(piece, off, 1) if off else piece
            lane = lax.broadcasted_iota(jnp.int32, (1, HD), 1)
            gains[n, row : row + 1, :] += jnp.where(lane >= off, moved, 0.0)
            if off + SLICE > HD:
                gains[n, row + 1 : row + 2, :] += jnp.where(lane < off + SLICE - HD, moved, 0.0)

    scale = 1.0 / math.sqrt(HD)
    along = (((1,), (1,)), ((), ()))
    down = (((0,), (0,)), ((), ()))
    plain = (((1,), (0,)), ((), ()))

    def dot(a, b, dims):
        return lax.dot_general(a, b, dims, preferred_element_type=F32)

    def mean(a):
        return jnp.sum(a, axis=-1, keepdims=True) * (1.0 / HD)

    def flat(ref, lo, hi):
        return ref[lo // TILE : hi // TILE].reshape(hi - lo, HD)

    def restore(raw, inv, gain, grad, n, h, lo):
        scaled = gain * grad
        normed = raw * inv
        out = inv * (scaled - normed * mean(normed * scaled))
        obuf[h, n, lo // TILE : (lo + BLK) // TILE] = out.astype(BF16).reshape(BF, TILE, HD)
        return jnp.sum(normed * grad, axis=0, keepdims=True)

    def head(h):
        done(recv.at[h], recv_sem.at[h])
        q_r, k_r, v_r, g_r = (recv.at[h, n] for n in range(4))
        gain_q = gains[0, pl.ds(h, 1), :]
        gain_k = gains[1, pl.ds(h, 1), :]
        inv_q, inv_k = [], []
        for b in range(NBLK):
            lo, hi = b * BLK, (b + 1) * BLK
            for src, invs, gain, dst in ((q_r, inv_q, gain_q, qh_s), (k_r, inv_k, gain_k, kh_s)):
                raw = flat(src, lo, hi).astype(F32)
                inv = lax.rsqrt(mean(raw * raw) + EPS)
                invs.append(inv)
                dst[lo:hi] = (raw * inv * gain).astype(BF16)

        part_q = jnp.zeros((1, HD), F32)
        part_k = jnp.zeros((1, HD), F32)
        for b in range(NBLK):
            lo, hi = b * BLK, (b + 1) * BLK
            scores = dot(kh_s[0:hi], qh_s[lo:hi], along)
            exps = jnp.exp(scores * scale + bias[0:hi, lo:hi])
            frame = (lax.broadcasted_iota(jnp.int32, (1, BLK), 1) + lo) // TILE
            dead = (frame >= length).astype(F32)
            total = jnp.sum(exps, axis=0, keepdims=True) + dead
            soft = exps * (1.0 / total)
            soft_b = soft.astype(BF16)
            dprob = dot(flat(v_r, 0, hi), flat(g_r, lo, hi), along)
            delta = jnp.sum(soft_b.astype(F32) * dprob, axis=0, keepdims=True)
            ds_b = (soft * (dprob - delta)).astype(BF16)
            soft_s[0:hi, lo:hi] = soft_b
            ds_s[0:hi, lo:hi] = ds_b
            dq = dot(ds_b, kh_s[0:hi], down) * scale
            raw = flat(q_r, lo, hi).astype(F32)
            part_q += restore(raw, inv_q[b], gain_q, dq, 0, h, lo)
        for b in range(NBLK):
            lo, hi = b * BLK, (b + 1) * BLK
            dk = dot(ds_s[lo:hi, lo:ROWS], qh_s[lo:ROWS], plain) * scale
            raw = flat(k_r, lo, hi).astype(F32)
            part_k += restore(raw, inv_k[b], gain_k, dk, 1, h, lo)
            dv = dot(soft_s[lo:hi, lo:ROWS], flat(g_r, lo, ROWS), plain)
            obuf[h, 2, lo // TILE : hi // TILE] = dv.astype(BF16).reshape(BF, TILE, HD)
        parts[0, pl.ds(h, 1), :] = part_q
        parts[1, pl.ds(h, 1), :] = part_k

        @pl.when(h < EARLY)
        def _():
            send_out(h)

    def send_out(h):
        place = o_ref.at[
            :, :, pl.ds(pl.multiple_of(j * TILE, TILE), TILE),
            pl.ds(pl.multiple_of((g * GH + h) * HD, HD), HD),
        ]
        for n in range(SEQ - 1):
            to = seq_peer(n)
            remote(
                obuf.at[h, :, pl.ds(to * OWN, OWN)], place, osend_sem, orecv_sem, (clip, to)
            )
        pltpu.make_async_copy(obuf.at[h, :, pl.ds(me * OWN, OWN)], place, orecv_sem).start()

    loop(0, GH, head)

    @pl.when(jnp.logical_not(agent))
    def _():
        remote(parts, parts_in.at[j - 1], pass_sem, pair_sem, (clip, me - j))

    send_out(EARLY)

    @pl.when(agent)
    def _():
        done(parts_in, pair_sem)
        parts[...] += jnp.sum(parts_in[...], axis=0)
        for zz in range(ZS):
            for n in range(2):
                psend[zz, n : n + 1, :] = lanes(lambda r: parts[n, r : r + 1, :], zz * SLICE)
        for d in range(1, ZS):
            zz = lax.rem(z + d, ZS)
            remote(psend.at[zz], precv.at[z], asend_sem, arecv_sem, at_z(zz))
        pltpu.make_async_copy(psend.at[z], precv.at[z], arecv_sem).start()

    send_out(EARLY + 1)

    @pl.when(agent)
    def _():
        done(precv, arecv_sem)
        asend[...] = jnp.sum(precv[...], axis=0)

    @pl.when(inner)
    def _():
        pltpu.make_async_copy(asend, brecv.at[x], brecv_sem).start()

    @pl.when(outer)
    def _():
        remote(asend, brecv.at[x], bsend_sem, brecv_sem, at_x(g))

    send_out(EARLY + 2)

    @pl.when(inner)
    def _():
        done(brecv, brecv_sem)
        csend[...] = jnp.sum(brecv[...], axis=0)
        for n in range(SEQ - 1):
            remote(csend, crecv.at[0], csend_sem, crecv_sem, (clip, seq_peer(n)))
        pltpu.make_async_copy(csend, crecv.at[0], crecv_sem).start()

    send_out(EARLY + 3)
    done(crecv.at[0], crecv_sem)
    gain_out[...] = crecv[0]

    @pl.when(inner)
    def _():
        done(brecv.at[pl.ds(0, XS - 1)], gsend_sem)
        done(crecv.at[pl.ds(0, SEQ - 1)], csend_sem)

    @pl.when(outer)
    def _():
        done(asend, bsend_sem)

    @pl.when(agent)
    def _():
        done(grecv.at[pl.ds(0, ZS - 1)], hsend_sem)
        done(precv.at[pl.ds(0, ZS - 1)], asend_sem)
        done(parts_in, pass_sem)

    @pl.when(jnp.logical_not(agent))
    def _():
        done(parts_in.at[0], pass_sem)

    done(recv.at[:, :, pl.ds(0, FRAMES - OWN)], send_sem)
    done(obuf.at[:, :, pl.ds(0, FRAMES - OWN)], osend_sem)
    done(o_ref, orecv_sem)


def unpack(o_ref, gain, out_q, out_k, out_v, gain_q, gain_k, line_q, line_k, sems):
    line_q[...] = gain[0:1, 0:SLICE]
    line_k[...] = gain[1:2, 0:SLICE]
    pairs = [(o_ref.at[n], ref) for n, ref in enumerate((out_q, out_k, out_v))]
    pairs += [(line_q, gain_q), (line_k, gain_k)]
    copies = [pltpu.make_async_copy(a, b, sems.at[n]) for n, (a, b) in enumerate(pairs)]
    for copy in copies:
        copy.start()
    for copy in copies:
        copy.wait()


def body(queries, key_rows, values, cotangent, lengths, episode_cuts, gain_q, gain_k):
    vmem = pl.BlockSpec(memory_space=pltpu.VMEM)
    hbm = pl.BlockSpec(memory_space=pltpu.HBM)
    dma = pltpu.SemaphoreType.DMA
    width = HEADS * HD
    row = pltpu.VMEM((2, HD), F32)
    out, gain = pl.pallas_call(
        kernel,
        out_shape=(
            pltpu.VMEM((3, OWN, PATCHES, width), BF16),
            pltpu.VMEM((2, HD), F32),
        ),
        in_specs=[pl.BlockSpec(memory_space=pltpu.SMEM)] + [hbm] * 7,
        out_specs=(vmem, vmem),
        scratch_shapes=[
            pltpu.SMEM((1, 2), jnp.int32),
            pltpu.VMEM((1, SLICE), F32),
            pltpu.VMEM((1, SLICE), F32),
            pltpu.VMEM((4, OWN, PATCHES, width), BF16),
            pltpu.VMEM((GH, 4, FRAMES, TILE, HD), BF16),
            pltpu.VMEM((GH, 3, FRAMES, TILE, HD), BF16),
            pltpu.VMEM((ROWS, HD), BF16),
            pltpu.VMEM((ROWS, HD), BF16),
            pltpu.VMEM((ROWS, ROWS), BF16),
            pltpu.VMEM((ROWS, ROWS), BF16),
            pltpu.VMEM((ROWS, ROWS), F32),
            pltpu.VMEM((2, 8, HD), F32),
            pltpu.VMEM((2, 8, HD), F32),
            row,
            row,
            pltpu.VMEM((ZS, 2, HD), F32),
            pltpu.VMEM((TILES - 1, 2, 8, HD), F32),
            pltpu.VMEM((ZS, 2, HD), F32),
            pltpu.VMEM((ZS, 2, HD), F32),
            row,
            pltpu.VMEM((XS, 2, HD), F32),
            row,
            pltpu.VMEM((SEQ, 2, HD), F32),
            pltpu.SemaphoreType.REGULAR,
            dma((3,)), dma, dma, dma((GH,)), dma, dma,
            dma, dma, dma, dma, dma, dma,
            dma, dma, dma, dma, dma, dma,
        ],
        compiler_params=pltpu.CompilerParams(
            collective_id=0, has_side_effects=True, vmem_limit_bytes=40 * 2**20
        ),
    )(
        lengths,
        *(
            pltpu.with_memory_space_constraint(a, pltpu.HBM)
            for a in (
                episode_cuts, gain_q.reshape(1, SLICE), gain_k.reshape(1, SLICE),
                *(a.reshape(OWN, PATCHES, width) for a in (queries, key_rows, values, cotangent)),
            )
        )
    )
    rows = pltpu.HBM((OWN, PATCHES, width), BF16)
    line = pltpu.HBM((1, SLICE), F32)
    *grads, grad_gq, grad_gk = pl.pallas_call(
        unpack,
        out_shape=(rows, rows, rows, line, line),
        in_specs=[vmem, vmem],
        out_specs=(hbm,) * 5,
        scratch_shapes=[pltpu.VMEM((1, SLICE), F32), pltpu.VMEM((1, SLICE), F32), dma((5,))],
    )(*(pltpu.with_memory_space_constraint(a, pltpu.VMEM) for a in (out, gain)))
    return (*(a[None] for a in grads), grad_gq.reshape(SLICE), grad_gk.reshape(SLICE))


def solution(mesh):
    rows = P("clip", "seq", None, None)
    return jax.shard_map(
        body,
        mesh=mesh,
        in_specs=(rows, rows, rows, rows, P("clip"), P("clip", None), P("clip"), P("clip")),
        out_specs=(rows, rows, rows, P("clip"), P("clip")),
        check_vma=False,
    )
```
